256 devices in a mesh: row: 8 (over z_hi, x), col: 32 (over z_lo, y, core).
Axes of the slice: x: 4, y: 4, z: 8 (z_hi: 2, z_lo: 4; z = z_hi * 4 + z_lo), core: 2. Of those that a mesh axis runs over, the one named last changes fastest.
Arguments:
- acts: bfloat16 [65536, 5120], P(('row', 'col')), may hold values from -24 to 24
- outgrads: bfloat16 [65536, 8192], P(('row', 'col')), may hold values from -24 to 24
- weight_grad: float32 [5120, 8192], P('row', 'col'), may hold values from -24 to 24
- prev_factor: float32 [256, 128, 128], P(('row', 'col')), as said below
- damping: float32 [], replicated, may hold values from 1 to 4
- block_slot_owner: int32 [256], replicated, may hold values from 0 to 255, each once
Outputs:
- precond_grad: float32 [5120, 8192], P('row', 'col')
- updated_factor_blocks: float32 [256, 128, 128], P(('row', 'col'))
The draws below stay inside these ranges and needn't reach their ends.
Inputs may be any that keep to these rules, and one draw needn't show every extreme that they name: `block_slot_owner`: A permutation of the 256 slots; only entries 0 to 103 name blocks' slots. `prev_factor`: symmetric blocks.
All inputs are finite; a program needn't handle non-finite values. Where the reference program divides by a largest or mean magnitude, that divisor is 1e-20 or more.
Results may differ from the reference program's by a relative error of at most 0.0003.
Values sent between devices are 32-bit elements; how exact they have to be, the bound alone decides.
No kernel may reach another device: no remote copies, remote signals or barrier semaphores. Data moves between devices by JAX's collectives and lax.ppermute only.
A program may use at most 128 MiB of HBM per device.

```python
import math
import jax
import jax.numpy as jnp
from jax import lax

D = 5120
H = 8192
BLOCK_ORDER = 128
ITERS = 6
TOKENS = 65536
NA = 40
NG = 64
NB = 104
FACTOR_SLOTS = 256


def draw_prev_factor(key, part):
    key = jax.random.fold_in(key, 7)
    first, second_factor = jax.random.split(key)
    block_shape = (FACTOR_SLOTS, BLOCK_ORDER, BLOCK_ORDER)
    diagonal_lower = 0.5
    diagonal_upper = 5.0
    raw = jax.random.normal(first, block_shape, jnp.float32)
    spread = 5.2 / BLOCK_ORDER
    symmetric = (raw + jnp.swapaxes(raw, 1, 2)) * (0.70710678 * spread)
    eye = jnp.eye(BLOCK_ORDER, dtype=jnp.float32)
    diagonal_entries = jnp.exp(jax.random.uniform(second_factor, (FACTOR_SLOTS, BLOCK_ORDER, 1), jnp.float32, jnp.log(diagonal_lower), jnp.log(diagonal_upper)))
    return symmetric * (1.0 - eye) + diagonal_entries * eye


def strengthened(drawn, stream_key, source, target, parts, factor):
    def block_of(axis_at):
        return (jnp.arange(drawn.shape[axis_at]) // (drawn.shape[axis_at] // parts)).reshape((-1,) + (1,) * (drawn.ndim - 1 - axis_at))

    first = jax.random.permutation(stream_key, parts)[block_of(target)]
    other_side = (block_of(target) + parts // 2) % parts
    return jnp.where((block_of(source) == first) | (block_of(source) == other_side), factor * drawn, drawn)


def block_scale(key, extent, pieces, low, high):
    def one(position, parts):
        heights = jax.random.uniform(jax.random.fold_in(jax.random.fold_in(key, 6), position), (parts,), jnp.float32, low / len(pieces), high / len(pieces))
        return jnp.repeat(jnp.exp(heights), extent[position] // parts).reshape((-1,) + (1,) * (len(extent) - position - 1))

    level = one(*pieces[0])
    for cut in pieces[1:]:
        level = level * one(*cut)
    return level


def normal_values(stream_key, extent, scale, reach, cuts=(), kind=jnp.bfloat16):
    values = jax.random.normal(stream_key, extent, jnp.float32) * scale
    if len(cuts) > 0:
        values = block_scale(stream_key, extent, cuts, -0.22, 0.18) * values
    return jnp.clip(values, min=-reach, max=reach).astype(kind)


def noise_with(rng, extent, deviation, limit, cuts, heavy, held_as=jnp.bfloat16):
    array = deviation * jax.random.normal(rng, extent, jnp.float32)
    if cuts:
        array = array * block_scale(rng, extent, cuts, -0.22, 0.18)
    return jnp.clip(strengthened(array, jax.random.fold_in(rng, 3), *heavy), -limit, limit).astype(held_as)


def setup_inputs(seed: int = 0) -> dict:
    key_list = jax.random.split(jax.random.key(seed), 7)
    return {
        "acts": noise_with(key_list[0], (TOKENS, D), 1.0, 24.0, ((0, 256),), (0, 1, 256, 6.0)),
        "outgrads": noise_with(key_list[1], (TOKENS, H), 1.0, 24.0, ((0, 256),), (0, 1, 256, 6.0)),
        "weight_grad": normal_values(key_list[2], (D, H), 4.0, 24.0, ((0, 8), (1, 32)), jnp.float32),
        "prev_factor": draw_prev_factor(jax.random.fold_in(key_list[6], 71), 0),
        "damping": jnp.clip(jnp.exp(jax.random.uniform(key_list[4], (), jnp.float32, math.log(1.0), math.log(4.0))), 1.0, 4.0),
        "block_slot_owner": jax.random.permutation(key_list[5], FACTOR_SLOTS).astype(jnp.int32),
    }


ema_decay = 0.8


def block_cov(data, count):
    def single(index):
        piece = lax.dynamic_slice_in_dim(data, index * BLOCK_ORDER, BLOCK_ORDER, 1)
        return jnp.dot(piece.T, piece, preferred_element_type=jnp.float32)
    return lax.map(single, jnp.arange(count, dtype=jnp.int32))


def invert(blocks, damp):
    eye = jnp.eye(blocks.shape[-1], dtype=jnp.float32)
    damped = blocks + damp * eye
    bound = jnp.max(jnp.sum(jnp.abs(damped), axis=2), axis=1)
    approx = eye[None] / bound[:, None, None]
    for step in range(ITERS):
        product = jnp.einsum("bij,bjk->bik", damped, approx, precision=lax.Precision.HIGHEST)
        approx = jnp.einsum("bij,bjk->bik", approx, 2.0 * eye - product, precision=lax.Precision.HIGHEST)
    return approx


def reference(acts, outgrads, weight_grad, prev_factor, damping, block_slot_owner):
    batch = jnp.concatenate([block_cov(acts, NA), block_cov(outgrads, NG)], axis=0) / TOKENS
    owner_slots = block_slot_owner[:NB]
    fresh_factor = ema_decay * prev_factor[owner_slots] + (1.0 - ema_decay) * batch
    updated_factor_blocks = jnp.zeros((FACTOR_SLOTS, BLOCK_ORDER, BLOCK_ORDER), jnp.float32).at[owner_slots].set(fresh_factor)
    inverse = invert(fresh_factor, damping)
    tiles = weight_grad.reshape(NA, BLOCK_ORDER, NG, BLOCK_ORDER)
    left = jnp.einsum("kij,kjlm->kilm", inverse[:NA], tiles, precision=lax.Precision.HIGHEST)
    both = jnp.einsum("kilm,lmn->kiln", left, inverse[NA:], precision=lax.Precision.HIGHEST)
    return both.reshape(D, H), updated_factor_blocks
```

```python
import functools

import jax
import jax.numpy as jnp
import numpy as np
from jax import lax
from jax.experimental import pallas as pl
from jax.experimental.pallas import tpu as pltpu
from jax.sharding import Mesh
from jax.sharding import PartitionSpec as P

D = 5120
H = 8192
N = 128
ITERS = 6
TOKENS = 65536
NA = D // N
NB = NA + H // N
SLOTS = 256

ema_decay = 0.8

HALF = 26
TILES = HALF + 1
ALL = ("zh", "x", "zl", "y", "c")
PLANE = ("x", "y")
DEPTH = ("zh", "zl")
SPREAD = ("c", "x", "y", "zh", "zl")


def pair_home(block):
    group, at = block // 10, (block % 10) // 2
    col = (block - NA) // 2
    last = at == 2
    high = at > 2
    a_half = jnp.where(last, group % 2, jnp.where(high, at - 3, at))
    a_place = jnp.where(last, 8 + group // 2, jnp.where(high, group + 4, group))
    is_a = block < NA
    return jnp.where(is_a, a_half, col % 2), jnp.where(is_a, a_place, 10 + col // 2)


def pair_column(place, half):
    if place < 8:
        return 0, 5 * (place % 4) + (3 if place >= 4 else 0) + half
    if place < 10:
        return 0, 5 * (half + 2 * (place - 8)) + 2
    return 1, 2 * (place - 10) + half


def lower_mask():
    r = lax.broadcasted_iota(jnp.int32, (N, N), 0)
    c = lax.broadcasted_iota(jnp.int32, (N, N), 1)
    return r, c


SCALE = (1.0 - ema_decay) / TOKENS


def gram(x):
    return lax.dot_general(x, x, (((0,), (0,)), ((), ())), preferred_element_type=jnp.float32)


def partial_kernel(own, meta, acts, outgrads, prev, diag_in, out, diag_out, buf, odd, rows, sems, odd_sems):
    half = meta[0]
    copies, odd_copies = [], []
    for place in range(HALF):
        which, pair = pair_column(place, half)
        src = outgrads if which else acts
        off = pl.multiple_of(pair * (2 * N), 2 * N)
        copies.append(pltpu.make_async_copy(src.at[:, pl.ds(off, 2 * N)], buf.at[place], sems.at[place]))
        copies[-1].start()
    if not own:
        for place in range(HALF):
            which, pair = pair_column(place, 1 - half)
            src = outgrads if which else acts
            off = pl.multiple_of(pair * (2 * N) + N, N)
            odd_copies.append(
                pltpu.make_async_copy(src.at[:, pl.ds(off, N)], odd.at[place], odd_sems.at[place])
            )
            odd_copies[-1].start()
        rows[...] = jnp.zeros((N, N), jnp.float32)
    r, c = lower_mask()
    for place in range(HALF):
        copies[place].wait()
        first = gram(buf[place, :, :N])
        second = gram(buf[place, :, N:])
        packed = jnp.where(r <= c, first, second) * SCALE
        out[:, place] = packed.reshape(16, 8, N)
        if not own:
            line = jnp.sum(jnp.where(r == c, second, 0.0), axis=0, keepdims=True)
            rows[pl.ds(32 * half + place, 1), :] = line * SCALE
    if not own:
        for place in range(HALF):
            odd_copies[place].wait()
            x = odd[place].astype(jnp.float32)
            rows[pl.ds(32 * (1 - half) + place, 1), :] = jnp.sum(x * x, axis=0, keepdims=True) * SCALE

    block, slot_half, place, second_of = meta[1], meta[2], meta[3], meta[4]

    @pl.when((block > 0) & (slot_half == half))
    def _():
        mine = jnp.where((r > c) == (second_of == 1), prev[0] * ema_decay, 0.0)
        out[:, place] += mine.reshape(16, 8, N)

    if own:
        out[:, HALF] = diag_in[...]
    else:

        @pl.when((block > 0) & (second_of == 1))
        def _():
            line = jnp.sum(jnp.where(r == c, prev[0], 0.0), axis=0, keepdims=True)
            rows[pl.ds(32 * slot_half + place, 1), :] += line * ema_decay

        diag = rows[...].T.reshape(16, 8, N)
        diag_out[...] = diag
        out[:, HALF] = diag


def partials(meta, acts, outgrads, prev, diag=None):
    own = diag is not None
    shape = jax.ShapeDtypeStruct((16, TILES, 8, N), jnp.float32)
    diag_shape = jax.ShapeDtypeStruct((16, 8, N), jnp.float32)
    vmem = pl.BlockSpec(memory_space=pltpu.VMEM)
    hbm = pl.BlockSpec(memory_space=pl.ANY)
    scratch = [pltpu.VMEM((HALF, 256, 2 * N), jnp.bfloat16)]
    if own:

        def kernel(meta, acts, outgrads, prev, diag_in, out, buf, sems):
            partial_kernel(True, meta, acts, outgrads, prev, diag_in, out, None, buf, None, None, sems, None)

        scratch += [pltpu.SemaphoreType.DMA((HALF,))]
    else:

        def kernel(meta, acts, outgrads, prev, out, diag_out, buf, odd, rows, sems, odd_sems):
            partial_kernel(
                False, meta, acts, outgrads, prev, None, out, diag_out, buf, odd, rows, sems, odd_sems
            )

        scratch += [
            pltpu.VMEM((HALF, 256, N), jnp.bfloat16),
            pltpu.VMEM((N, N), jnp.float32),
            pltpu.SemaphoreType.DMA((HALF,)),
            pltpu.SemaphoreType.DMA((HALF,)),
        ]
    return pl.pallas_call(
        kernel,
        out_shape=shape if own else (shape, diag_shape),
        in_specs=[pl.BlockSpec(memory_space=pltpu.SMEM), hbm, hbm, vmem] + ([vmem] if own else []),
        out_specs=vmem if own else (vmem, vmem),
        scratch_shapes=scratch,
        compiler_params=pltpu.CompilerParams(vmem_limit_bytes=40 * 2**20),
        name="own_half" if own else "other_half",
    )(*((meta, acts, outgrads, prev) + ((diag,) if own else ())))


def plane_kernel(got, out, total):
    for tile in range(TILES):
        parts = [got[s, tile] for s in range(16)]
        while len(parts) > 1:
            parts = [a + b for a, b in zip(parts[::2], parts[1::2])]
        total[pl.ds(8 * tile, 8), :] = parts[0]
    total[pl.ds(8 * TILES, 40), :] = jnp.zeros((40, N), jnp.float32)
    for z in range(8):
        out[z] = total[pl.ds(z, 32, stride=8), :]


def plane_sum(got):
    return pl.pallas_call(
        plane_kernel,
        out_shape=jax.ShapeDtypeStruct((8, 32, N), jnp.float32),
        in_specs=[pl.BlockSpec(memory_space=pltpu.VMEM)],
        out_specs=pl.BlockSpec(memory_space=pltpu.VMEM),
        scratch_shapes=[pltpu.VMEM((256, N), jnp.float32)],
        compiler_params=pltpu.CompilerParams(vmem_limit_bytes=40 * 2**20),
        name="plane_sum",
    )(got)


def thirds(x):
    high = x.astype(jnp.bfloat16)
    rest = x - high.astype(jnp.float32)
    mid = rest.astype(jnp.bfloat16)
    low = (rest - mid.astype(jnp.float32)).astype(jnp.bfloat16)
    return high, mid, low


def spread_kernel(got, picks, out):
    total = got[0]
    for z in range(1, 8):
        total = total + got[z]
    stacked = jnp.concatenate(thirds(total), axis=0)
    out[...] = jnp.dot(picks[...], stacked, preferred_element_type=jnp.float32)


def spread_rows(got, picks):
    return pl.pallas_call(
        spread_kernel,
        out_shape=jax.ShapeDtypeStruct((4 * SLOTS, N), jnp.float32),
        in_specs=[pl.BlockSpec(memory_space=pltpu.VMEM)] * 2,
        out_specs=pl.BlockSpec(memory_space=pltpu.VMEM),
        compiler_params=pltpu.CompilerParams(vmem_limit_bytes=40 * 2**20),
        name="spread_rows",
    )(got, picks)


def left_form(a):
    a1, a2, a3 = thirds(a)
    return jnp.concatenate([a1, a2], axis=1), jnp.concatenate([a1, a3], axis=1)


def mul(left, b):
    b1, b2, b3 = thirds(b)
    wide = jnp.concatenate(
        [jnp.concatenate([b1, b2], axis=1), jnp.concatenate([b2, b1], axis=1)], axis=0
    )
    main = jnp.dot(left[0], wide, preferred_element_type=jnp.float32)
    small = jnp.dot(left[1], jnp.concatenate([b3, b1], axis=0), preferred_element_type=jnp.float32)
    return main[:, :N] + (main[:, N:] + small)


def apply_kernel(meta, got, damping, weight, out, updated, left_out):
    core, row, col = meta[0], meta[1], meta[2]
    block, slot_half, slot_place, slot_second = meta[3], meta[4], meta[5], meta[6]
    group, odd_row = row // 2, row % 2
    r, c = lower_mask()
    lower, on = r > c, r == c
    eye = jnp.where(on, 1.0, 0.0)

    def fetch(half, k):
        return got[pl.ds(half * 512 + k, N, stride=4), :]

    diags = fetch(1 - core, 2)

    def block_of(packed, flipped, second, lane):
        column = jnp.sum(jnp.where(c == lane, diags, 0.0), axis=1, keepdims=True)
        if isinstance(second, int):
            if second == 0:
                return jnp.where(lower, flipped, packed)
            return jnp.where(on, column, jnp.where(lower, packed, flipped))
        straight = jnp.where(lower, second, 1 - second) == 1
        return jnp.where(on & (second == 1), column, jnp.where(straight, packed, flipped))

    blocks = []
    for half in range(2):
        packed = fetch(half, 0)
        flipped = packed.T
        lane = 32 * half + group + 4 * odd_row
        blocks += [block_of(packed, flipped, second, lane) for second in range(2)]
    packed = fetch(group % 2, 1)
    blocks.append(block_of(packed, packed.T, odd_row, 32 * (group % 2) + 8 + group // 2))
    packed = fetch(core, 2)
    flipped = packed.T
    blocks += [block_of(packed, flipped, second, 32 * core + 10 + col // 2) for second in range(2)]
    packed = fetch(slot_half, 3)
    fresh = block_of(packed, packed.T, slot_second, 32 * slot_half + slot_place)
    updated[0] = jnp.where(block > 0, fresh, 0.0)

    damped, approx = [], []
    for one in blocks:
        one = one + damping[0] * eye
        bound = jnp.max(jnp.sum(jnp.abs(one), axis=0, keepdims=True), axis=1, keepdims=True)
        start = 1.0 / bound
        damped.append(left_form(one))
        approx.append((2.0 * eye - one * start) * start)
    for _ in range(ITERS - 1):
        rest = [2.0 * eye - mul(d, x) for d, x in zip(damped, approx)]
        approx = [mul(left_form(x), y) for x, y in zip(approx, rest)]

    for i in range(5):
        place = jnp.where(odd_row == 1, (i + 1) % 5, i)
        at = pl.ds(pl.multiple_of(place * N, N), N)
        a = left_form(approx[i])
        w1, w2, w3 = thirds(weight[at, :])
        main = jnp.dot(a[0], jnp.concatenate([w1, w1], axis=0), preferred_element_type=jnp.float32)
        a1, a2 = a[0][:, :N], a[0][:, N:]
        a3 = a[1][:, N:]
        cross = jnp.dot(a[0], jnp.concatenate([w2, w2], axis=0), preferred_element_type=jnp.float32)
        small = jnp.dot(
            jnp.concatenate([a1, a3], axis=1),
            jnp.concatenate([w3, w1], axis=0),
            preferred_element_type=jnp.float32,
        )
        left_out[at, :] = main + (cross + small)
    for j in range(2):
        at = slice(j * N, (j + 1) * N)
        out[:, at] = mul(left_form(left_out[:, at]), approx[5 + j])


def apply_all(meta, got, damping, weight):
    vmem = pl.BlockSpec(memory_space=pltpu.VMEM)
    smem = pl.BlockSpec(memory_space=pltpu.SMEM)
    return pl.pallas_call(
        apply_kernel,
        out_shape=(
            jax.ShapeDtypeStruct(weight.shape, jnp.float32),
            jax.ShapeDtypeStruct((1, N, N), jnp.float32),
        ),
        in_specs=[smem, vmem, smem, vmem],
        out_specs=(vmem, vmem),
        scratch_shapes=[pltpu.VMEM(weight.shape, jnp.float32)],
        compiler_params=pltpu.CompilerParams(vmem_limit_bytes=40 * 2**20),
        name="invert_apply",
    )(meta, got, damping, weight)


def destinations():
    c, x, y, zh, zl = np.unravel_index(np.arange(SLOTS), (2, 4, 4, 2, 4))
    row, col = zh * 4 + x, (zl * 4 + y) * 2 + c
    return c, row, col, row * 32 + col


def picked_rows(owner, half):
    core, row, col, slot = destinations()
    group, odd_row = row // 2, row % 2
    first = group + 4 * odd_row
    second = 8 + group // 2
    third = jnp.where(jnp.asarray(core) == half, jnp.asarray(10 + col // 2), HALF)
    halves, places = pair_home(jnp.arange(NB, dtype=jnp.int32))
    matches = (owner[:NB, None] == jnp.asarray(slot, jnp.int32)[None, :]) & (halves == half)[:, None]
    fourth = jnp.sum(jnp.where(matches, places[:, None], 0), axis=0)
    rows = jnp.stack([jnp.asarray(first), jnp.asarray(second), third, fourth], axis=1).astype(jnp.int32)
    wanted = jnp.arange(96, dtype=jnp.int32) % 32
    return (rows[:, :, None] == wanted).astype(jnp.bfloat16).reshape(4 * SLOTS, 96)


def on_device(acts, outgrads, weight_grad, prev_factor, damping, owner):
    core = lax.axis_index("c").astype(jnp.int32)
    row = lax.axis_index(("zh", "x")).astype(jnp.int32)
    col = lax.axis_index(("zl", "y", "c")).astype(jnp.int32)
    me = row * 32 + col
    numbers = jnp.arange(NB, dtype=jnp.int32)
    block = jnp.sum(jnp.where(owner[:NB] == me, numbers + 1, 0))
    slot_half, slot_place = pair_home(jnp.maximum(block - 1, 0))
    slot_second = jnp.maximum(block - 1, 0) % 2
    slot = [block, slot_half, slot_place, slot_second]
    other_meta = jnp.stack([1 - core] + slot).astype(jnp.int32)
    own_meta = jnp.stack([core] + slot).astype(jnp.int32)
    apply_meta = jnp.stack([core, row, col] + slot).astype(jnp.int32)
    picks = picked_rows(owner, core)

    other, diag = partials(other_meta, acts, outgrads, prev_factor)
    received = lax.ppermute(other, "c", [(0, 1), (1, 0)])
    own = partials(own_meta, acts, outgrads, prev_factor, diag)
    chip = own + received
    got = lax.all_to_all(chip, PLANE, 0, 0, tiled=True)
    by_depth = plane_sum(got)
    got = lax.all_to_all(by_depth, DEPTH, 0, 0, tiled=True)
    sent = spread_rows(got, picks)
    got = lax.all_to_all(sent.reshape(SLOTS, 4, N), SPREAD, 0, 0, tiled=True)
    return apply_all(apply_meta, got.reshape(4 * SLOTS, N), damping.reshape(1), weight_grad)


def solution(mesh):
    fine = Mesh(mesh.devices.reshape(2, 4, 4, 4, 2), ALL)
    row, col = ("zh", "x"), ("zl", "y", "c")
    placed = (P(ALL, None), P(ALL, None), P(row, col), P(ALL, None, None), P(), P())
    return jax.shard_map(
        on_device,
        mesh=fine,
        in_specs=placed,
        out_specs=(P(row, col), P(ALL, None, None)),
        check_vma=False,
    )
```

```python
import functools

import jax
import jax.numpy as jnp
import numpy as np
from jax import lax
from jax.experimental import pallas as pl
from jax.experimental.pallas import tpu as pltpu
from jax.sharding import Mesh
from jax.sharding import PartitionSpec as P

D = 5120
H = 8192
N = 128
ITERS = 6
TOKENS = 65536
NA = D // N
NB = NA + H // N
SLOTS = 256

ema_decay = 0.8

HALF = 26
TILES = HALF + 1
ALL = ("zh", "x", "zl", "y", "c")
PLANE = ("x", "y")
DEPTH = ("zh", "zl")
SPREAD = ("c", "x", "y", "zh", "zl")


def pair_home(block):
    group, at = block // 10, (block % 10) // 2
    col = (block - NA) // 2
    last = at == 2
    high = at > 2
    a_half = jnp.where(last, group % 2, jnp.where(high, at - 3, at))
    a_place = jnp.where(last, 8 + group // 2, jnp.where(high, group + 4, group))
    is_a = block < NA
    return jnp.where(is_a, a_half, col % 2), jnp.where(is_a, a_place, 10 + col // 2)


def pair_column(place, half):
    if place < 8:
        return 0, 5 * (place % 4) + (3 if place >= 4 else 0) + half
    if place < 10:
        return 0, 5 * (half + 2 * (place - 8)) + 2
    return 1, 2 * (place - 10) + half


def lower_mask():
    r = lax.broadcasted_iota(jnp.int32, (N, N), 0)
    c = lax.broadcasted_iota(jnp.int32, (N, N), 1)
    return r, c


SCALE = (1.0 - ema_decay) / TOKENS


def gram(x):
    return lax.dot_general(x, x, (((0,), (0,)), ((), ())), preferred_element_type=jnp.float32)


GROUPS = (12, 14)


def partial_kernel(core_of, me_of, own, *refs):
    if own:
        acts, outgrads, prev_hbm, owner_hbm, diag_in, out, buf, prev, owner, sems, small_sems = refs
    else:
        acts, outgrads, prev_hbm, owner_hbm, out_hbm, diag_out = refs[:6]
        buf, prev, owner, sems, small_sems, out, out_sems, odd, rows, odd_sems = refs[6:]
    core, me = core_of(), me_of()
    half = core if own else 1 - core
    small = [
        pltpu.make_async_copy(owner_hbm, owner, small_sems.at[0]),
        pltpu.make_async_copy(prev_hbm, prev, small_sems.at[1]),
    ]
    small[0].start()
    copies, odd_copies = [], []
    for place in range(HALF):
        which, pair = pair_column(place, half)
        off = pl.multiple_of(pair * (2 * N), 2 * N)
        src = (outgrads if which else acts).at[:, pl.ds(off, 2 * N)]
        copies.append(pltpu.make_async_copy(src, buf.at[place], sems.at[place]))
        copies[-1].start()
    small[1].start()
    r, c = lower_mask()
    if not own:
        for place in range(HALF):
            which, pair = pair_column(place, core)
            off = pl.multiple_of(pair * (2 * N) + N, N)
            src = (outgrads if which else acts).at[:, pl.ds(off, N)]
            odd_copies.append(pltpu.make_async_copy(src, odd.at[place], odd_sems.at[place]))
            odd_copies[-1].start()
        rows[...] = jnp.zeros((N, N), jnp.float32)

    small[0].wait()
    block = jnp.int32(0)
    for i in range(NB):
        block = jnp.where(owner[i] == me, i + 1, block)
    slot = jnp.maximum(block - 1, 0)
    slot_half, slot_place = pair_home(slot)
    second_of = slot % 2

    done, sent = 0, []
    for number, count in enumerate(GROUPS):
        begin, end = done, done + count
        done = end
        for place in range(begin, end):
            copies[place].wait()
        for place in range(begin, end):
            first = gram(buf[place, :, :N])
            second = gram(buf[place, :, N:])
            packed = jnp.where(r <= c, first, second) * SCALE
            out[:, place] = packed.reshape(16, 8, N)
            if not own:
                line = jnp.sum(jnp.where(r == c, second, 0.0), axis=0, keepdims=True)
                rows[pl.ds(32 * half + place, 1), :] = line * SCALE
        if number == 0:
            small[1].wait()

        @pl.when((block > 0) & (slot_half == half) & (slot_place >= begin) & (slot_place < end))
        def _():
            mine = jnp.where((r > c) == (second_of == 1), prev[0] * ema_decay, 0.0)
            out[:, slot_place] += mine.reshape(16, 8, N)

        if not own:
            at = pl.ds(begin, count)
            sent.append(pltpu.make_async_copy(out.at[:, at], out_hbm.at[:, at], out_sems.at[number]))
            sent[-1].start()
    if own:
        out[:, HALF] = diag_in[...]
        return
    for place in range(HALF):
        odd_copies[place].wait()
    for place in range(HALF):
        x = odd[place].astype(jnp.float32)
        rows[pl.ds(32 * core + place, 1), :] = jnp.sum(x * x, axis=0, keepdims=True) * SCALE

    @pl.when((block > 0) & (second_of == 1))
    def _():
        line = jnp.sum(jnp.where(r == c, prev[0], 0.0), axis=0, keepdims=True)
        rows[pl.ds(32 * slot_half + slot_place, 1), :] += line * ema_decay

    diag = rows[...].T.reshape(16, 8, N)
    diag_out[...] = diag
    out[:, HALF] = diag
    at = pl.ds(HALF, 1)
    sent.append(pltpu.make_async_copy(out.at[:, at], out_hbm.at[:, at], out_sems.at[len(GROUPS)]))
    sent[-1].start()
    for copy in sent:
        copy.wait()


def partials(acts, outgrads, prev, owner, core_of, me_of, diag=None):
    own = diag is not None
    shape = jax.ShapeDtypeStruct((16, TILES, 8, N), jnp.float32)
    diag_shape = jax.ShapeDtypeStruct((16, 8, N), jnp.float32)
    hbm, vmem = pl.BlockSpec(memory_space=pltpu.HBM), pl.BlockSpec(memory_space=pltpu.VMEM)
    scratch = [
        pltpu.VMEM((HALF, 256, 2 * N), jnp.bfloat16),
        pltpu.VMEM((1, N, N), jnp.float32),
        pltpu.SMEM((SLOTS,), jnp.int32),
        pltpu.SemaphoreType.DMA((HALF,)),
        pltpu.SemaphoreType.DMA((2,)),
    ]
    if not own:
        scratch += [
            pltpu.VMEM((16, TILES, 8, N), jnp.float32),
            pltpu.SemaphoreType.DMA((len(GROUPS) + 1,)),
            pltpu.VMEM((HALF, 256, N), jnp.bfloat16),
            pltpu.VMEM((N, N), jnp.float32),
            pltpu.SemaphoreType.DMA((HALF,)),
        ]
    return pl.pallas_call(
        functools.partial(partial_kernel, core_of, me_of, own),
        out_shape=shape if own else (shape, diag_shape),
        in_specs=[hbm] * 4 + ([vmem] if own else []),
        out_specs=vmem if own else (hbm, vmem),
        scratch_shapes=scratch,
        compiler_params=pltpu.CompilerParams(vmem_limit_bytes=(50 if own else 61) * 2**20),
        name="own_half" if own else "other_half",
    )(*((acts, outgrads, prev, owner) + ((diag,) if own else ())))


CHUNKS = 4


def add_kernel(own, received, out_hbm, out, sems):
    copies = []
    for i in range(CHUNKS):
        at = pl.ds(i * (16 // CHUNKS), 16 // CHUNKS)
        out[at] = own[at] + received[at]
        copies.append(pltpu.make_async_copy(out.at[at], out_hbm.at[at], sems.at[i]))
        copies[-1].start()
    for copy in copies:
        copy.wait()


def add_cores(own, received):
    hbm, vmem = pl.BlockSpec(memory_space=pltpu.HBM), pl.BlockSpec(memory_space=pltpu.VMEM)
    return pl.pallas_call(
        add_kernel,
        out_shape=jax.ShapeDtypeStruct(own.shape, jnp.float32),
        in_specs=[vmem, vmem],
        out_specs=hbm,
        scratch_shapes=[pltpu.VMEM(own.shape, jnp.float32), pltpu.SemaphoreType.DMA((CHUNKS,))],
        compiler_params=pltpu.CompilerParams(vmem_limit_bytes=16 * 2**20),
        name="add_cores",
    )(own, received)


def plane_kernel(got, out, total):
    for tile in range(TILES):
        parts = [got[s, pl.ds(8 * tile, 8), :] for s in range(16)]
        while len(parts) > 1:
            parts = [a + b for a, b in zip(parts[::2], parts[1::2])]
        total[pl.ds(8 * tile, 8), :] = parts[0]
    total[pl.ds(8 * TILES, 40), :] = jnp.zeros((40, N), jnp.float32)
    for z in range(8):
        out[z] = total[pl.ds(z, 32, stride=8), :]


def plane_sum(got):
    return pl.pallas_call(
        plane_kernel,
        out_shape=jax.ShapeDtypeStruct((8, 32, N), jnp.float32),
        in_specs=[pl.BlockSpec(memory_space=pltpu.VMEM)],
        out_specs=pl.BlockSpec(memory_space=pltpu.VMEM),
        scratch_shapes=[pltpu.VMEM((256, N), jnp.float32)],
        compiler_params=pltpu.CompilerParams(vmem_limit_bytes=40 * 2**20),
        name="plane_sum",
    )(got)


def thirds(x):
    high = x.astype(jnp.bfloat16)
    rest = x - high.astype(jnp.float32)
    mid = rest.astype(jnp.bfloat16)
    low = (rest - mid.astype(jnp.float32)).astype(jnp.bfloat16)
    return high, mid, low


def spread_kernel(got, picks, out):
    total = got[0]
    for z in range(1, 8):
        total = total + got[z]
    stacked = jnp.concatenate(thirds(total), axis=0)
    out[...] = jnp.dot(picks[...], stacked, preferred_element_type=jnp.float32)


def spread_rows(got, picks):
    return pl.pallas_call(
        spread_kernel,
        out_shape=jax.ShapeDtypeStruct((4 * SLOTS, N), jnp.float32),
        in_specs=[pl.BlockSpec(memory_space=pltpu.VMEM)] * 2,
        out_specs=pl.BlockSpec(memory_space=pltpu.VMEM),
        compiler_params=pltpu.CompilerParams(vmem_limit_bytes=40 * 2**20),
        name="spread_rows",
    )(got, picks)


def left_form(a):
    a1, a2, a3 = thirds(a)
    return jnp.concatenate([a1, a2], axis=1), jnp.concatenate([a1, a3], axis=1)


def mul(left, b):
    b1, b2, b3 = thirds(b)
    wide = jnp.concatenate(
        [jnp.concatenate([b1, b2], axis=1), jnp.concatenate([b2, b1], axis=1)], axis=0
    )
    main = jnp.dot(left[0], wide, preferred_element_type=jnp.float32)
    small = jnp.dot(left[1], jnp.concatenate([b3, b1], axis=0), preferred_element_type=jnp.float32)
    return main[:, :N] + (main[:, N:] + small)


def apply_kernel(meta, got, damping, weight, out, updated, left_out):
    core, row, col = meta[0], meta[1], meta[2]
    block, slot_half, slot_place, slot_second = meta[3], meta[4], meta[5], meta[6]
    group, odd_row = row // 2, row % 2
    r, c = lower_mask()
    lower, on = r > c, r == c
    eye = jnp.where(on, 1.0, 0.0)

    def fetch(half, k):
        return got[pl.ds(half * 512 + k, N, stride=4), :]

    diags = fetch(1 - core, 2)

    def block_of(packed, flipped, second, lane):
        column = jnp.sum(jnp.where(c == lane, diags, 0.0), axis=1, keepdims=True)
        if isinstance(second, int):
            if second == 0:
                return jnp.where(lower, flipped, packed)
            return jnp.where(on, column, jnp.where(lower, packed, flipped))
        straight = jnp.where(lower, second, 1 - second) == 1
        return jnp.where(on & (second == 1), column, jnp.where(straight, packed, flipped))

    blocks = []
    for half in range(2):
        packed = fetch(half, 0)
        flipped = packed.T
        lane = 32 * half + group + 4 * odd_row
        blocks += [block_of(packed, flipped, second, lane) for second in range(2)]
    packed = fetch(group % 2, 1)
    blocks.append(block_of(packed, packed.T, odd_row, 32 * (group % 2) + 8 + group // 2))
    packed = fetch(core, 2)
    flipped = packed.T
    blocks += [block_of(packed, flipped, second, 32 * core + 10 + col // 2) for second in range(2)]
    packed = fetch(slot_half, 3)
    fresh = block_of(packed, packed.T, slot_second, 32 * slot_half + slot_place)
    updated[0] = jnp.where(block > 0, fresh, 0.0)

    damped, approx = [], []
    for one in blocks:
        one = one + damping[0] * eye
        bound = jnp.max(jnp.sum(jnp.abs(one), axis=0, keepdims=True), axis=1, keepdims=True)
        start = 1.0 / bound
        damped.append(left_form(one))
        approx.append((2.0 * eye - one * start) * start)
    for _ in range(ITERS - 1):
        rest = [2.0 * eye - mul(d, x) for d, x in zip(damped, approx)]
        approx = [mul(left_form(x), y) for x, y in zip(approx, rest)]

    for i in range(5):
        place = jnp.where(odd_row == 1, (i + 1) % 5, i)
        at = pl.ds(pl.multiple_of(place * N, N), N)
        a = left_form(approx[i])
        w1, w2, w3 = thirds(weight[at, :])
        main = jnp.dot(a[0], jnp.concatenate([w1, w1], axis=0), preferred_element_type=jnp.float32)
        a1, a2 = a[0][:, :N], a[0][:, N:]
        a3 = a[1][:, N:]
        cross = jnp.dot(a[0], jnp.concatenate([w2, w2], axis=0), preferred_element_type=jnp.float32)
        small = jnp.dot(
            jnp.concatenate([a1, a3], axis=1),
            jnp.concatenate([w3, w1], axis=0),
            preferred_element_type=jnp.float32,
        )
        left_out[at, :] = main + (cross + small)
    for j in range(2):
        at = slice(j * N, (j + 1) * N)
        out[:, at] = mul(left_form(left_out[:, at]), approx[5 + j])


def apply_all(meta, got, damping, weight):
    vmem = pl.BlockSpec(memory_space=pltpu.VMEM)
    smem = pl.BlockSpec(memory_space=pltpu.SMEM)
    return pl.pallas_call(
        apply_kernel,
        out_shape=(
            jax.ShapeDtypeStruct(weight.shape, jnp.float32),
            jax.ShapeDtypeStruct((1, N, N), jnp.float32),
        ),
        in_specs=[smem, vmem, smem, vmem],
        out_specs=(vmem, vmem),
        scratch_shapes=[pltpu.VMEM(weight.shape, jnp.float32)],
        compiler_params=pltpu.CompilerParams(vmem_limit_bytes=40 * 2**20),
        name="invert_apply",
    )(meta, got, damping, weight)


def destinations():
    c, x, y, zh, zl = np.unravel_index(np.arange(SLOTS), (2, 4, 4, 2, 4))
    row, col = zh * 4 + x, (zl * 4 + y) * 2 + c
    return c, row, col, row * 32 + col


def picked_rows(owner, half):
    core, row, col, slot = destinations()
    group, odd_row = row // 2, row % 2
    first = group + 4 * odd_row
    second = 8 + group // 2
    third = jnp.where(jnp.asarray(core) == half, jnp.asarray(10 + col // 2), HALF)
    halves, places = pair_home(jnp.arange(NB, dtype=jnp.int32))
    matches = (owner[:NB, None] == jnp.asarray(slot, jnp.int32)[None, :]) & (halves == half)[:, None]
    fourth = jnp.sum(jnp.where(matches, places[:, None], 0), axis=0)
    rows = jnp.stack([jnp.asarray(first), jnp.asarray(second), third, fourth], axis=1).astype(jnp.int32)
    wanted = jnp.arange(96, dtype=jnp.int32) % 32
    return (rows[:, :, None] == wanted).astype(jnp.bfloat16).reshape(4 * SLOTS, 96)


def on_device(acts, outgrads, weight_grad, prev_factor, damping, owner):
    core_of = lambda: lax.axis_index("c").astype(jnp.int32)
    row_of = lambda: lax.axis_index(("zh", "x")).astype(jnp.int32)
    col_of = lambda: lax.axis_index(("zl", "y", "c")).astype(jnp.int32)
    me_of = lambda: row_of() * 32 + col_of()

    other, diag = partials(acts, outgrads, prev_factor, owner, core_of, me_of)
    received = lax.ppermute(other, "c", [(0, 1), (1, 0)])
    own = partials(acts, outgrads, prev_factor, owner, core_of, me_of, diag)
    chip = add_cores(own, received)

    owner, _ = lax.optimization_barrier((owner, other))
    core, row, col, me = core_of(), row_of(), col_of(), me_of()
    numbers = jnp.arange(NB, dtype=jnp.int32)
    block = jnp.sum(jnp.where(owner[:NB] == me, numbers + 1, 0))
    slot_half, slot_place = pair_home(jnp.maximum(block - 1, 0))
    slot_second = jnp.maximum(block - 1, 0) % 2
    slot = [block, slot_half, slot_place, slot_second]
    apply_meta = jnp.stack([core, row, col] + slot).astype(jnp.int32)
    picks = picked_rows(owner, core)

    got = lax.all_to_all(chip.reshape(16, 8 * TILES, N), PLANE, 0, 0, tiled=True)
    by_depth = plane_sum(got)
    got = lax.all_to_all(by_depth, DEPTH, 0, 0, tiled=True)
    sent = spread_rows(got, picks)
    got = lax.all_to_all(sent.reshape(SLOTS, 4, N), SPREAD, 0, 0, tiled=True)
    return apply_all(apply_meta, got.reshape(4 * SLOTS, N), damping.reshape(1), weight_grad)


def solution(mesh):
    fine = Mesh(mesh.devices.reshape(2, 4, 4, 4, 2), ALL)
    row, col = ("zh", "x"), ("zl", "y", "c")
    placed = (P(ALL, None), P(ALL, None), P(row, col), P(ALL, None, None), P(), P())
    return jax.shard_map(
        on_device,
        mesh=fine,
        in_specs=placed,
        out_specs=(P(row, col), P(ALL, None, None)),
        check_vma=False,
    )
```

```python
import functools

import jax
import jax.numpy as jnp
import numpy as np
from jax import lax
from jax.experimental import pallas as pl
from jax.experimental.pallas import tpu as pltpu
from jax.sharding import Mesh
from jax.sharding import PartitionSpec as P

D = 5120
H = 8192
N = 128
ITERS = 6
TOKENS = 65536
NA = D // N
NB = NA + H // N
SLOTS = 256

ema_decay = 0.8

HALF = 26
TILES = HALF + 1
ALL = ("zh", "x", "zl", "y", "c")
PLANE = ("x", "y")
DEPTH = ("zh", "zl")
CHIPS = ("x", "y", "zh", "zl")
ROWS = 6


def pair_home(block):
    group, at = block // 10, (block % 10) // 2
    col = (block - NA) // 2
    last = at == 2
    high = at > 2
    a_half = jnp.where(last, group % 2, jnp.where(high, at - 3, at))
    a_place = jnp.where(last, 8 + group // 2, jnp.where(high, group + 4, group))
    is_a = block < NA
    return jnp.where(is_a, a_half, col % 2), jnp.where(is_a, a_place, 10 + col // 2)


def pair_column(place, half):
    if place < 8:
        return 0, 5 * (place % 4) + (3 if place >= 4 else 0) + half
    if place < 10:
        return 0, 5 * (half + 2 * (place - 8)) + 2
    return 1, 2 * (place - 10) + half


def lower_mask():
    r = lax.broadcasted_iota(jnp.int32, (N, N), 0)
    c = lax.broadcasted_iota(jnp.int32, (N, N), 1)
    return r, c


SCALE = (1.0 - ema_decay) / TOKENS


def gram(x):
    return lax.dot_general(x, x, (((0,), (0,)), ((), ())), preferred_element_type=jnp.float32)


GROUPS = (12, 14)


def partial_kernel(core_of, me_of, own, *refs):
    if own:
        acts, outgrads, prev_hbm, owner_hbm, out, buf, prev, owner, rows, sems, small_sems = refs
    else:
        acts, outgrads, prev_hbm, owner_hbm, out_hbm, buf, prev, owner, rows, sems, small_sems, out, out_sems = refs
    core, me = core_of(), me_of()
    half = core if own else 1 - core
    small = [
        pltpu.make_async_copy(owner_hbm, owner, small_sems.at[0]),
        pltpu.make_async_copy(prev_hbm, prev, small_sems.at[1]),
    ]
    small[0].start()
    copies = []
    for place in range(HALF):
        which, pair = pair_column(place, half)
        off = pl.multiple_of(pair * (2 * N), 2 * N)
        src = (outgrads if which else acts).at[:, pl.ds(off, 2 * N)]
        copies.append(pltpu.make_async_copy(src, buf.at[place], sems.at[place]))
        copies[-1].start()
    small[1].start()
    r, c = lower_mask()
    rows[...] = jnp.zeros((N, N), jnp.float32)

    small[0].wait()
    block = jnp.int32(0)
    for i in range(NB):
        block = jnp.where(owner[i] == me, i + 1, block)
    slot = jnp.maximum(block - 1, 0)
    slot_half, slot_place = pair_home(slot)
    second_of = slot % 2

    done, sent = 0, []
    for number, count in enumerate(GROUPS):
        begin, end = done, done + count
        done = end
        for place in range(begin, end):
            copies[place].wait()
        for place in range(begin, end):
            first = gram(buf[place, :, :N])
            second = gram(buf[place, :, N:])
            packed = jnp.where(r <= c, first, second) * SCALE
            out[:, place] = packed.reshape(16, 8, N)
            line = jnp.sum(jnp.where(r == c, second, 0.0), axis=0, keepdims=True)
            rows[pl.ds(32 * half + place, 1), :] = line * SCALE
        if number == 0:
            small[1].wait()

        @pl.when((block > 0) & (slot_half == half) & (slot_place >= begin) & (slot_place < end))
        def _():
            mine = jnp.where((r > c) == (second_of == 1), prev[0] * ema_decay, 0.0)
            out[:, slot_place] += mine.reshape(16, 8, N)

        at = pl.ds(begin, count)
        if end == HALF:

            @pl.when((block > 0) & (slot_half == half) & (second_of == 1))
            def _():
                line = jnp.sum(jnp.where(r == c, prev[0], 0.0), axis=0, keepdims=True)
                rows[pl.ds(32 * half + slot_place, 1), :] += line * ema_decay

            out[:, HALF] = rows[...].T.reshape(16, 8, N)
            at = pl.ds(begin, count + 1)
        if not own:
            sent.append(pltpu.make_async_copy(out.at[:, at], out_hbm.at[:, at], out_sems.at[number]))
            sent[-1].start()
    for copy in sent:
        copy.wait()


def partials(acts, outgrads, prev, owner, core_of, me_of, own):
    hbm, vmem = pl.BlockSpec(memory_space=pltpu.HBM), pl.BlockSpec(memory_space=pltpu.VMEM)
    scratch = [
        pltpu.VMEM((HALF, 256, 2 * N), jnp.bfloat16),
        pltpu.VMEM((1, N, N), jnp.float32),
        pltpu.SMEM((SLOTS,), jnp.int32),
        pltpu.VMEM((N, N), jnp.float32),
        pltpu.SemaphoreType.DMA((HALF,)),
        pltpu.SemaphoreType.DMA((2,)),
    ]
    if not own:
        scratch += [
            pltpu.VMEM((16, TILES, 8, N), jnp.float32),
            pltpu.SemaphoreType.DMA((len(GROUPS),)),
        ]
    return pl.pallas_call(
        functools.partial(partial_kernel, core_of, me_of, own),
        out_shape=jax.ShapeDtypeStruct((16, TILES, 8, N), jnp.float32),
        in_specs=[hbm] * 4,
        out_specs=vmem if own else hbm,
        scratch_shapes=scratch,
        compiler_params=pltpu.CompilerParams(vmem_limit_bytes=(50 if own else 61) * 2**20),
        name="own_half" if own else "other_half",
    )(acts, outgrads, prev, owner)


CHUNKS = 4


def add_kernel(own, received, out_hbm, out, sems):
    copies = []
    for i in range(CHUNKS):
        at = pl.ds(i * (16 // CHUNKS), 16 // CHUNKS)
        out[at] = own[at] + received[at]
        copies.append(pltpu.make_async_copy(out.at[at], out_hbm.at[at], sems.at[i]))
        copies[-1].start()
    for copy in copies:
        copy.wait()


def add_cores(own, received):
    hbm, vmem = pl.BlockSpec(memory_space=pltpu.HBM), pl.BlockSpec(memory_space=pltpu.VMEM)
    return pl.pallas_call(
        add_kernel,
        out_shape=jax.ShapeDtypeStruct(own.shape, jnp.float32),
        in_specs=[vmem, vmem],
        out_specs=hbm,
        scratch_shapes=[pltpu.VMEM(own.shape, jnp.float32), pltpu.SemaphoreType.DMA((CHUNKS,))],
        compiler_params=pltpu.CompilerParams(vmem_limit_bytes=16 * 2**20),
        name="add_cores",
    )(own, received)


def plane_kernel(got, out, total):
    for tile in range(TILES):
        parts = [got[s, pl.ds(8 * tile, 8), :] for s in range(16)]
        while len(parts) > 1:
            parts = [a + b for a, b in zip(parts[::2], parts[1::2])]
        total[pl.ds(8 * tile, 8), :] = parts[0]
    total[pl.ds(8 * TILES, 40), :] = jnp.zeros((40, N), jnp.float32)
    for z in range(8):
        out[z] = total[pl.ds(z, 32, stride=8), :]


def plane_sum(got):
    return pl.pallas_call(
        plane_kernel,
        out_shape=jax.ShapeDtypeStruct((8, 32, N), jnp.float32),
        in_specs=[pl.BlockSpec(memory_space=pltpu.VMEM)],
        out_specs=pl.BlockSpec(memory_space=pltpu.VMEM),
        scratch_shapes=[pltpu.VMEM((256, N), jnp.float32)],
        compiler_params=pltpu.CompilerParams(vmem_limit_bytes=40 * 2**20),
        name="plane_sum",
    )(got)


def thirds(x):
    high = x.astype(jnp.bfloat16)
    rest = x - high.astype(jnp.float32)
    mid = rest.astype(jnp.bfloat16)
    low = (rest - mid.astype(jnp.float32)).astype(jnp.bfloat16)
    return high, mid, low


def spread_kernel(got, picks, out):
    total = got[0]
    for z in range(1, 8):
        total = total + got[z]
    stacked = jnp.concatenate(thirds(total), axis=0)
    out[...] = jnp.dot(picks[...], stacked, preferred_element_type=jnp.float32)


def spread_rows(got, picks):
    return pl.pallas_call(
        spread_kernel,
        out_shape=jax.ShapeDtypeStruct((ROWS * N, N), jnp.float32),
        in_specs=[pl.BlockSpec(memory_space=pltpu.VMEM)] * 2,
        out_specs=pl.BlockSpec(memory_space=pltpu.VMEM),
        compiler_params=pltpu.CompilerParams(vmem_limit_bytes=40 * 2**20),
        name="spread_rows",
    )(got, picks)


def left_form(a):
    a1, a2, a3 = thirds(a)
    return jnp.concatenate([a1, a2], axis=1), jnp.concatenate([a1, a3], axis=1)


def mul(left, b):
    b1, b2, b3 = thirds(b)
    wide = jnp.concatenate(
        [jnp.concatenate([b1, b2], axis=1), jnp.concatenate([b2, b1], axis=1)], axis=0
    )
    main = jnp.dot(left[0], wide, preferred_element_type=jnp.float32)
    small = jnp.dot(left[1], jnp.concatenate([b3, b1], axis=0), preferred_element_type=jnp.float32)
    return main[:, :N] + (main[:, N:] + small)


def unpacked(packed, second, diags, lane):
    r, c = lower_mask()
    lower, on = r > c, r == c
    flipped = packed.T
    if isinstance(second, int) and second == 0:
        return jnp.where(lower, flipped, packed)
    column = jnp.sum(jnp.where(c == lane, diags, 0.0), axis=1, keepdims=True)
    if isinstance(second, int):
        return jnp.where(on, column, jnp.where(lower, packed, flipped))
    straight = jnp.where(lower, second, 1 - second) == 1
    return jnp.where(on & (second == 1), column, jnp.where(straight, packed, flipped))


def inverses(blocks, damping):
    r, c = lower_mask()
    eye = jnp.where(r == c, 1.0, 0.0)
    damped, approx = [], []
    for one in blocks:
        one = one + damping * eye
        bound = jnp.max(jnp.sum(jnp.abs(one), axis=0, keepdims=True), axis=1, keepdims=True)
        start = 1.0 / bound
        damped.append(left_form(one))
        approx.append((2.0 * eye - one * start) * start)
    for _ in range(ITERS - 1):
        rest = [2.0 * eye - mul(d, x) for d, x in zip(damped, approx)]
        approx = [mul(left_form(x), y) for x, y in zip(approx, rest)]
    return approx


def both_sides(left, w, right):
    a12, a13 = left_form(left)
    a1 = a12[:, :N]
    w1, w2, w3 = thirds(w)
    main = jnp.dot(a12, jnp.concatenate([w1, w1], axis=0), preferred_element_type=jnp.float32)
    cross = jnp.dot(a12, jnp.concatenate([w2, w2], axis=0), preferred_element_type=jnp.float32)
    small = jnp.dot(
        jnp.concatenate([a1, a13[:, N:]], axis=1),
        jnp.concatenate([w3, w1], axis=0),
        preferred_element_type=jnp.float32,
    )
    product = main + (cross + small)
    return jnp.concatenate([mul(left_form(product[:, j * N : (j + 1) * N]), right[j]) for j in range(2)], axis=1)


def group_rows(index, odd_row):
    place = 4 * (1 - odd_row) if isinstance(index, str) else index + odd_row
    return pl.ds(pl.multiple_of(place * N, N), N)


def near_kernel(meta, own, damping, weight, rows_out, right_out):
    core, row, col = meta[0], meta[1], meta[2]
    group, odd_row = row // 2, row % 2

    def fetch(k):
        return own[pl.ds(k, N, stride=ROWS), :]

    diags, first, last = fetch(3), fetch(0), fetch(2)
    lane = 32 * core + group + 4 * odd_row
    blocks = [unpacked(first, second, diags, lane) for second in range(2)]
    blocks += [unpacked(last, second, diags, 32 * core + 10 + col // 2) for second in range(2)]
    approx = inverses(blocks, damping[0])
    for i in range(2):
        rows_out[pl.ds(i * N, N), :] = both_sides(approx[i], weight[group_rows(2 * core + i, odd_row), :], approx[2:])
        right_out[i] = approx[2 + i]


def far_kernel(meta, own, other, damping, weight, rows_in, right_in, out, updated):
    core, row = meta[0], meta[1]
    block, slot_half, slot_place, slot_second = meta[3], meta[4], meta[5], meta[6]
    group, odd_row = row // 2, row % 2
    fifth_half = group % 2

    def fetch(ref, k):
        return ref[pl.ds(k, N, stride=ROWS), :]

    diags = fetch(own, 3) + fetch(other, 3)
    first = fetch(other, 0)
    fifth = jnp.where(fifth_half == core, fetch(own, 1), fetch(other, 1))
    lane = 32 * (1 - core) + group + 4 * odd_row
    blocks = [unpacked(first, second, diags, lane) for second in range(2)]
    blocks.append(unpacked(fifth, odd_row, diags, 32 * fifth_half + 8 + group // 2))
    mine = jnp.where(slot_half == core, fetch(own, 4 + core), fetch(other, 4 + core))
    fresh = unpacked(mine, slot_second, diags, 32 * slot_half + slot_place)
    updated[0] = jnp.where(block > 0, fresh, 0.0)

    approx = inverses(blocks, damping[0])
    right = [right_in[0], right_in[1]]
    for i in range(2):
        out[group_rows(2 * core + i, odd_row), :] = rows_in[pl.ds(i * N, N), :]
        at = group_rows(2 * (1 - core) + i, odd_row)
        out[at, :] = both_sides(approx[i], weight[at, :], right)
    at = group_rows("fifth", odd_row)
    out[at, :] = both_sides(approx[2], weight[at, :], right)


def apply_near(meta, own, damping, weight):
    vmem, smem = pl.BlockSpec(memory_space=pltpu.VMEM), pl.BlockSpec(memory_space=pltpu.SMEM)
    return pl.pallas_call(
        near_kernel,
        out_shape=(
            jax.ShapeDtypeStruct((2 * N, 2 * N), jnp.float32),
            jax.ShapeDtypeStruct((2, N, N), jnp.float32),
        ),
        in_specs=[smem, vmem, smem, vmem],
        out_specs=(vmem, vmem),
        compiler_params=pltpu.CompilerParams(vmem_limit_bytes=40 * 2**20),
        name="apply_near",
    )(meta, own, damping, weight)


def apply_far(meta, own, other, damping, weight, rows, right):
    vmem, smem = pl.BlockSpec(memory_space=pltpu.VMEM), pl.BlockSpec(memory_space=pltpu.SMEM)
    return pl.pallas_call(
        far_kernel,
        out_shape=(
            jax.ShapeDtypeStruct(weight.shape, jnp.float32),
            jax.ShapeDtypeStruct((1, N, N), jnp.float32),
        ),
        in_specs=[smem, vmem, vmem, smem, vmem, vmem, vmem],
        out_specs=(vmem, vmem),
        compiler_params=pltpu.CompilerParams(vmem_limit_bytes=40 * 2**20),
        name="apply_far",
    )(meta, own, other, damping, weight, rows, right)


def picked_rows(owner, half):
    x, y, zh, zl = np.unravel_index(np.arange(N), (4, 4, 2, 4))
    row, pair_col = zh * 4 + x, zl * 4 + y
    group, odd_row = row // 2, row % 2
    fixed = [group + 4 * odd_row, 8 + group // 2, 10 + pair_col, np.full(N, HALF)]
    halves, places = pair_home(jnp.arange(NB, dtype=jnp.int32))
    slots = []
    for core in range(2):
        slot = jnp.asarray(row * 32 + pair_col * 2 + core, jnp.int32)
        matches = (owner[:NB, None] == slot[None, :]) & (halves == half)[:, None]
        slots.append(jnp.sum(jnp.where(matches, places[:, None], 0), axis=0))
    rows = jnp.stack([jnp.asarray(f) for f in fixed] + slots, axis=1).astype(jnp.int32)
    wanted = jnp.arange(96, dtype=jnp.int32) % 32
    return (rows[:, :, None] == wanted).astype(jnp.bfloat16).reshape(ROWS * N, 96)


def on_device(acts, outgrads, weight_grad, prev_factor, damping, owner):
    core_of = lambda: lax.axis_index("c").astype(jnp.int32)
    row_of = lambda: lax.axis_index(("zh", "x")).astype(jnp.int32)
    col_of = lambda: lax.axis_index(("zl", "y", "c")).astype(jnp.int32)
    me_of = lambda: row_of() * 32 + col_of()

    swap = [(0, 1), (1, 0)]
    other = partials(acts, outgrads, prev_factor, owner, core_of, me_of, False)
    received = lax.ppermute(other, "c", swap)
    own = partials(acts, outgrads, prev_factor, owner, core_of, me_of, True)
    chip = add_cores(own, received)

    owner, _ = lax.optimization_barrier((owner, other))
    core, row, col, me = core_of(), row_of(), col_of(), me_of()
    numbers = jnp.arange(NB, dtype=jnp.int32)
    block = jnp.sum(jnp.where(owner[:NB] == me, numbers + 1, 0))
    slot_half, slot_place = pair_home(jnp.maximum(block - 1, 0))
    slot_second = jnp.maximum(block - 1, 0) % 2
    slot = [block, slot_half, slot_place, slot_second]
    apply_meta = jnp.stack([core, row, col] + slot).astype(jnp.int32)
    picks = picked_rows(owner, core)

    got = lax.all_to_all(chip.reshape(16, 8 * TILES, N), PLANE, 0, 0, tiled=True)
    by_depth = plane_sum(got)
    got = lax.all_to_all(by_depth, DEPTH, 0, 0, tiled=True)
    damping = damping.reshape(1)
    got, apply_meta, damping = lax.optimization_barrier((got, apply_meta, damping))
    sent = spread_rows(got, picks)
    near = lax.all_to_all(sent.reshape(N, ROWS, 1, N), CHIPS, 0, 0, tiled=True).reshape(ROWS * N, N)
    far = lax.ppermute(near, "c", swap)
    rows, right = apply_near(apply_meta, near, damping, weight_grad)
    return apply_far(apply_meta, near, far, damping, weight_grad, rows, right)


def solution(mesh):
    fine = Mesh(mesh.devices.reshape(2, 4, 4, 4, 2), ALL)
    row, col = ("zh", "x"), ("zl", "y", "c")
    placed = (P(ALL, None), P(ALL, None), P(row, col), P(ALL, None, None), P(), P())
    return jax.shard_map(
        on_device,
        mesh=fine,
        in_specs=placed,
        out_specs=(P(row, col), P(ALL, None, None)),
        check_vma=False,
    )
```

```python
import functools

import jax
import jax.numpy as jnp
import numpy as np
from jax import lax
from jax.experimental import pallas as pl
from jax.experimental.pallas import tpu as pltpu
from jax.sharding import Mesh
from jax.sharding import PartitionSpec as P

D = 5120
H = 8192
N = 128
ITERS = 6
TOKENS = 65536
NA = D // N
NB = NA + H // N
SLOTS = 256

ema_decay = 0.8

HALF = 26
TILES = HALF + 1
ALL = ("zh", "x", "zl", "y", "c")
PLANE = ("x", "y")
DEPTH = ("zh", "zl")
CHIPS = ("x", "y", "zh", "zl")
ROWS = 6


def pair_home(block):
    group, at = block // 10, (block % 10) // 2
    col = (block - NA) // 2
    last = at == 2
    high = at > 2
    a_half = jnp.where(last, group % 2, jnp.where(high, at - 3, at))
    a_place = jnp.where(last, 8 + group // 2, jnp.where(high, group + 4, group))
    is_a = block < NA
    return jnp.where(is_a, a_half, col % 2), jnp.where(is_a, a_place, 10 + col // 2)


def pair_column(place, half):
    if place < 8:
        return 0, 5 * (place % 4) + (3 if place >= 4 else 0) + half
    if place < 10:
        return 0, 5 * (half + 2 * (place - 8)) + 2
    return 1, 2 * (place - 10) + half


def lower_mask():
    r = lax.broadcasted_iota(jnp.int32, (N, N), 0)
    c = lax.broadcasted_iota(jnp.int32, (N, N), 1)
    return r, c


SCALE = (1.0 - ema_decay) / TOKENS


def gram(x):
    return lax.dot_general(x, x, (((0,), (0,)), ((), ())), preferred_element_type=jnp.float32)


GROUPS = (12, 14)


def partial_kernel(core_of, me_of, own, *refs):
    if own:
        acts, outgrads, prev_hbm, owner_hbm, out, buf, prev, owner, rows, sems, small_sems = refs
    else:
        acts, outgrads, prev_hbm, owner_hbm, out_hbm, buf, prev, owner, rows, sems, small_sems, out, out_sems = refs
    core, me = core_of(), me_of()
    half = core if own else 1 - core
    small = [
        pltpu.make_async_copy(owner_hbm, owner, small_sems.at[0]),
        pltpu.make_async_copy(prev_hbm, prev, small_sems.at[1]),
    ]
    small[0].start()
    copies = []
    for place in range(HALF):
        which, pair = pair_column(place, half)
        off = pl.multiple_of(pair * (2 * N), 2 * N)
        src = (outgrads if which else acts).at[:, pl.ds(off, 2 * N)]
        copies.append(pltpu.make_async_copy(src, buf.at[place], sems.at[place]))
        copies[-1].start()
    small[1].start()
    r, c = lower_mask()
    rows[...] = jnp.zeros((N, N), jnp.float32)

    small[0].wait()
    block = jnp.int32(0)
    for i in range(NB):
        block = jnp.where(owner[i] == me, i + 1, block)
    slot = jnp.maximum(block - 1, 0)
    slot_half, slot_place = pair_home(slot)
    second_of = slot % 2

    done, sent = 0, []
    for number, count in enumerate(GROUPS):
        begin, end = done, done + count
        done = end
        for place in range(begin, end):
            copies[place].wait()
        for place in range(begin, end):
            first = gram(buf[place, :, :N])
            second = gram(buf[place, :, N:])
            packed = jnp.where(r <= c, first, second) * SCALE
            out[:, place] = packed.reshape(16, 8, N)
            line = jnp.sum(jnp.where(r == c, second, 0.0), axis=0, keepdims=True)
            rows[pl.ds(32 * half + place, 1), :] = line * SCALE
        if number == 0:
            small[1].wait()

        @pl.when((block > 0) & (slot_half == half) & (slot_place >= begin) & (slot_place < end))
        def _():
            mine = jnp.where((r > c) == (second_of == 1), prev[0] * ema_decay, 0.0)
            out[:, slot_place] += mine.reshape(16, 8, N)

        at = pl.ds(begin, count)
        if end == HALF:

            @pl.when((block > 0) & (slot_half == half) & (second_of == 1))
            def _():
                line = jnp.sum(jnp.where(r == c, prev[0], 0.0), axis=0, keepdims=True)
                rows[pl.ds(32 * half + slot_place, 1), :] += line * ema_decay

            out[:, HALF] = rows[...].T.reshape(16, 8, N)
            at = pl.ds(begin, count + 1)
        if not own:
            sent.append(pltpu.make_async_copy(out.at[:, at], out_hbm.at[:, at], out_sems.at[number]))
            sent[-1].start()
    for copy in sent:
        copy.wait()


def partials(acts, outgrads, prev, owner, core_of, me_of, own):
    hbm, vmem = pl.BlockSpec(memory_space=pltpu.HBM), pl.BlockSpec(memory_space=pltpu.VMEM)
    scratch = [
        pltpu.VMEM((HALF, 256, 2 * N), jnp.bfloat16),
        pltpu.VMEM((1, N, N), jnp.float32),
        pltpu.SMEM((SLOTS,), jnp.int32),
        pltpu.VMEM((N, N), jnp.float32),
        pltpu.SemaphoreType.DMA((HALF,)),
        pltpu.SemaphoreType.DMA((2,)),
    ]
    if not own:
        scratch += [
            pltpu.VMEM((16, TILES, 8, N), jnp.float32),
            pltpu.SemaphoreType.DMA((len(GROUPS),)),
        ]
    return pl.pallas_call(
        functools.partial(partial_kernel, core_of, me_of, own),
        out_shape=jax.ShapeDtypeStruct((16, TILES, 8, N), jnp.float32),
        in_specs=[hbm] * 4,
        out_specs=vmem if own else hbm,
        scratch_shapes=scratch,
        compiler_params=pltpu.CompilerParams(vmem_limit_bytes=(50 if own else 61) * 2**20),
        name="own_half" if own else "other_half",
    )(acts, outgrads, prev, owner)


CHUNKS = 4


def add_kernel(own, received, out_hbm, out, sems):
    copies = []
    for i in range(CHUNKS):
        at = pl.ds(i * (16 // CHUNKS), 16 // CHUNKS)
        out[at] = own[at] + received[at]
        copies.append(pltpu.make_async_copy(out.at[at], out_hbm.at[at], sems.at[i]))
        copies[-1].start()
    for copy in copies:
        copy.wait()


def add_cores(own, received):
    hbm, vmem = pl.BlockSpec(memory_space=pltpu.HBM), pl.BlockSpec(memory_space=pltpu.VMEM)
    return pl.pallas_call(
        add_kernel,
        out_shape=jax.ShapeDtypeStruct(own.shape, jnp.float32),
        in_specs=[vmem, vmem],
        out_specs=hbm,
        scratch_shapes=[pltpu.VMEM(own.shape, jnp.float32), pltpu.SemaphoreType.DMA((CHUNKS,))],
        compiler_params=pltpu.CompilerParams(vmem_limit_bytes=16 * 2**20),
        name="add_cores",
    )(own, received)


def plane_kernel(got, out, total):
    for tile in range(TILES):
        parts = [got[s, pl.ds(8 * tile, 8), :] for s in range(16)]
        while len(parts) > 1:
            parts = [a + b for a, b in zip(parts[::2], parts[1::2])]
        total[pl.ds(8 * tile, 8), :] = parts[0]
    total[pl.ds(8 * TILES, 40), :] = jnp.zeros((40, N), jnp.float32)
    for z in range(8):
        out[z] = total[pl.ds(z, 32, stride=8), :]


def plane_sum(got):
    return pl.pallas_call(
        plane_kernel,
        out_shape=jax.ShapeDtypeStruct((8, 32, N), jnp.float32),
        in_specs=[pl.BlockSpec(memory_space=pltpu.VMEM)],
        out_specs=pl.BlockSpec(memory_space=pltpu.VMEM),
        scratch_shapes=[pltpu.VMEM((256, N), jnp.float32)],
        compiler_params=pltpu.CompilerParams(vmem_limit_bytes=40 * 2**20),
        name="plane_sum",
    )(got)


def thirds(x):
    high = x.astype(jnp.bfloat16)
    rest = x - high.astype(jnp.float32)
    mid = rest.astype(jnp.bfloat16)
    low = (rest - mid.astype(jnp.float32)).astype(jnp.bfloat16)
    return high, mid, low


def spread_kernel(got, picks, out):
    total = got[0]
    for z in range(1, 8):
        total = total + got[z]
    stacked = jnp.concatenate(thirds(total), axis=0)
    out[...] = jnp.dot(picks[...], stacked, preferred_element_type=jnp.float32)


def spread_rows(got, picks):
    return pl.pallas_call(
        spread_kernel,
        out_shape=jax.ShapeDtypeStruct((ROWS * N, N), jnp.float32),
        in_specs=[pl.BlockSpec(memory_space=pltpu.VMEM)] * 2,
        out_specs=pl.BlockSpec(memory_space=pltpu.VMEM),
        compiler_params=pltpu.CompilerParams(vmem_limit_bytes=40 * 2**20),
        name="spread_rows",
    )(got, picks)


def halves(x):
    high = x.astype(jnp.bfloat16)
    return high, (x - high.astype(jnp.float32)).astype(jnp.bfloat16)


def left_form(a):
    return jnp.concatenate(halves(a), axis=1)


def right_form(b):
    b1, b2 = halves(b)
    return jnp.concatenate([jnp.concatenate([b1, b2], axis=1), jnp.concatenate([b2, b1], axis=1)], axis=0)


def times(left, right):
    four = jnp.dot(left, right, preferred_element_type=jnp.float32)
    return four[:, :N] + four[:, N:]


def mul(left, b):
    return times(left, right_form(b))


def square(e):
    e1 = e.astype(jnp.bfloat16)
    low = e - e1.astype(jnp.float32)
    e2 = low.astype(jnp.bfloat16)
    e3 = (low - e2.astype(jnp.float32)).astype(jnp.bfloat16)
    wide = jnp.concatenate([jnp.concatenate([e1, e2], axis=1), jnp.concatenate([e2, e1], axis=1)], axis=0)
    four = jnp.dot(jnp.concatenate([e1, e2], axis=1), wide, preferred_element_type=jnp.float32)
    two = jnp.dot(
        jnp.concatenate([e1, e3], axis=1), jnp.concatenate([e3, e1], axis=0), preferred_element_type=jnp.float32
    )
    return four[:, :N] + (four[:, N:] + two)


def unpacked(packed, second, diags, lane):
    r, c = lower_mask()
    lower, on = r > c, r == c
    flipped = packed.T
    if isinstance(second, int) and second == 0:
        return jnp.where(lower, flipped, packed)
    column = jnp.sum(jnp.where(c == lane, diags, 0.0), axis=1, keepdims=True)
    if isinstance(second, int):
        return jnp.where(on, column, jnp.where(lower, packed, flipped))
    straight = jnp.where(lower, second, 1 - second) == 1
    return jnp.where(on & (second == 1), column, jnp.where(straight, packed, flipped))


def inverses(blocks, damping):
    r, c = lower_mask()
    eye = jnp.where(r == c, 1.0, 0.0)
    rest, approx = [], []
    for one in blocks:
        one = one + damping * eye
        bound = jnp.max(jnp.sum(jnp.abs(one), axis=0, keepdims=True), axis=1, keepdims=True)
        start = 1.0 / bound
        rest.append(eye - one * start)
        approx.append((eye + rest[-1]) * start)
    right = None
    for step in range(ITERS - 1):
        if step < 2:
            rest = [square(e) for e in rest]
        else:
            rest = [times(left_form(e), f) for e, f in zip(rest, right)]
        right = [right_form(e) for e in rest]
        approx = [x + times(left_form(x), f) for x, f in zip(approx, right)]
    return approx


def both_sides(left, w, right):
    left = left_form(left)
    parts = []
    for j in range(2):
        product = mul(left, w[:, j * N : (j + 1) * N])
        parts.append(times(left_form(product), right[j]))
    return jnp.concatenate(parts, axis=1)


def group_rows(index, odd_row):
    place = 4 * (1 - odd_row) if isinstance(index, str) else index + odd_row
    return pl.ds(pl.multiple_of(place * N, N), N)


def number(meta, i):
    return meta[i].astype(jnp.int32)


def near_kernel(meta, own, weight, rows_out, right_out):
    core, row, col = [number(meta, i) for i in range(3)]
    damping = meta[7]
    group, odd_row = row // 2, row % 2

    def fetch(k):
        return own[pl.ds(k, N, stride=ROWS), :]

    diags, first, last = fetch(3), fetch(0), fetch(2)
    lane = 32 * core + group + 4 * odd_row
    blocks = [unpacked(first, second, diags, lane) for second in range(2)]
    blocks += [unpacked(last, second, diags, 32 * core + 10 + col // 2) for second in range(2)]
    approx = inverses(blocks, damping)
    right = [right_form(one) for one in approx[2:]]
    for i in range(2):
        rows_out[pl.ds(i * N, N), :] = both_sides(approx[i], weight[group_rows(2 * core + i, odd_row), :], right)
        right_out[i] = right[i]


def far_kernel(meta, own, other, weight, rows_in, right_in, out_hbm, updated_hbm, out, updated, sems):
    core, row = number(meta, 0), number(meta, 1)
    block, slot_half, slot_place, slot_second = [number(meta, i) for i in range(3, 7)]
    damping = meta[7]
    group, odd_row = row // 2, row % 2
    fifth_half = group % 2
    sent = []

    def send(src, dst):
        sent.append(pltpu.make_async_copy(src, dst, sems.at[len(sent)]))
        sent[-1].start()

    for i in range(2):
        send(rows_in.at[pl.ds(i * N, N), :], out_hbm.at[group_rows(2 * core + i, odd_row), :])

    def fetch(ref, k):
        return ref[pl.ds(k, N, stride=ROWS), :]

    diags = fetch(own, 3) + fetch(other, 3)
    first = fetch(other, 0)
    fifth = jnp.where(fifth_half == core, fetch(own, 1), fetch(other, 1))
    lane = 32 * (1 - core) + group + 4 * odd_row
    blocks = [unpacked(first, second, diags, lane) for second in range(2)]
    blocks.append(unpacked(fifth, odd_row, diags, 32 * fifth_half + 8 + group // 2))
    mine = jnp.where(slot_half == core, fetch(own, 4 + core), fetch(other, 4 + core))
    fresh = unpacked(mine, slot_second, diags, 32 * slot_half + slot_place)
    updated[0] = jnp.where(block > 0, fresh, 0.0)
    send(updated, updated_hbm)

    approx = inverses(blocks, damping)
    right = [right_in[0], right_in[1]]
    for i in range(3):
        at = group_rows("fifth" if i == 2 else 2 * (1 - core) + i, odd_row)
        out[pl.ds(i * N, N), :] = both_sides(approx[i], weight[at, :], right)
        send(out.at[pl.ds(i * N, N), :], out_hbm.at[at, :])
    for copy in sent:
        copy.wait()


def apply_near(meta, own, weight):
    vmem, smem = pl.BlockSpec(memory_space=pltpu.VMEM), pl.BlockSpec(memory_space=pltpu.SMEM)
    return pl.pallas_call(
        near_kernel,
        out_shape=(
            jax.ShapeDtypeStruct((2 * N, 2 * N), jnp.float32),
            jax.ShapeDtypeStruct((2, 2 * N, 2 * N), jnp.bfloat16),
        ),
        in_specs=[smem, vmem, vmem],
        out_specs=(vmem, vmem),
        compiler_params=pltpu.CompilerParams(vmem_limit_bytes=40 * 2**20),
        name="apply_near",
    )(meta, own, weight)


def apply_far(meta, own, other, weight, rows, right):
    vmem, smem = pl.BlockSpec(memory_space=pltpu.VMEM), pl.BlockSpec(memory_space=pltpu.SMEM)
    hbm = pl.BlockSpec(memory_space=pltpu.HBM)
    return pl.pallas_call(
        far_kernel,
        out_shape=(
            jax.ShapeDtypeStruct(weight.shape, jnp.float32),
            jax.ShapeDtypeStruct((1, N, N), jnp.float32),
        ),
        in_specs=[smem] + [vmem] * 5,
        out_specs=(hbm, hbm),
        scratch_shapes=[
            pltpu.VMEM((3 * N, 2 * N), jnp.float32),
            pltpu.VMEM((1, N, N), jnp.float32),
            pltpu.SemaphoreType.DMA((6,)),
        ],
        compiler_params=pltpu.CompilerParams(vmem_limit_bytes=40 * 2**20),
        name="apply_far",
    )(meta, own, other, weight, rows, right)


def picked_rows(owner, half):
    x, y, zh, zl = np.unravel_index(np.arange(N), (4, 4, 2, 4))
    row, pair_col = zh * 4 + x, zl * 4 + y
    group, odd_row = row // 2, row % 2
    fixed = [group + 4 * odd_row, 8 + group // 2, 10 + pair_col, np.full(N, HALF)]
    halves, places = pair_home(jnp.arange(NB, dtype=jnp.int32))
    slots = []
    for core in range(2):
        slot = jnp.asarray(row * 32 + pair_col * 2 + core, jnp.int32)
        matches = (owner[:NB, None] == slot[None, :]) & (halves == half)[:, None]
        slots.append(jnp.sum(jnp.where(matches, places[:, None], 0), axis=0))
    rows = jnp.stack([jnp.asarray(f) for f in fixed] + slots, axis=1).astype(jnp.int32)
    wanted = jnp.arange(96, dtype=jnp.int32) % 32
    return (rows[:, :, None] == wanted).astype(jnp.bfloat16).reshape(ROWS * N, 96)


def on_device(acts, outgrads, weight_grad, prev_factor, damping, owner):
    core_of = lambda: lax.axis_index("c").astype(jnp.int32)
    row_of = lambda: lax.axis_index(("zh", "x")).astype(jnp.int32)
    col_of = lambda: lax.axis_index(("zl", "y", "c")).astype(jnp.int32)
    me_of = lambda: row_of() * 32 + col_of()

    swap = [(0, 1), (1, 0)]
    other = partials(acts, outgrads, prev_factor, owner, core_of, me_of, False)
    received = lax.ppermute(other, "c", swap)
    own = partials(acts, outgrads, prev_factor, owner, core_of, me_of, True)
    chip = add_cores(own, received)

    owner, _ = lax.optimization_barrier((owner, other))
    core, row, col, me = core_of(), row_of(), col_of(), me_of()
    numbers = jnp.arange(NB, dtype=jnp.int32)
    block = jnp.sum(jnp.where(owner[:NB] == me, numbers + 1, 0))
    slot_half, slot_place = pair_home(jnp.maximum(block - 1, 0))
    slot_second = jnp.maximum(block - 1, 0) % 2
    slot = [block, slot_half, slot_place, slot_second]
    apply_meta = jnp.stack([one.astype(jnp.float32) for one in [core, row, col] + slot + [damping]])
    picks = picked_rows(owner, core)

    got = lax.all_to_all(chip.reshape(16, 8 * TILES, N), PLANE, 0, 0, tiled=True)
    by_depth = plane_sum(got)
    got = lax.all_to_all(by_depth, DEPTH, 0, 0, tiled=True)
    got, apply_meta = lax.optimization_barrier((got, apply_meta))
    sent = spread_rows(got, picks)
    near = lax.all_to_all(sent.reshape(N, ROWS, 1, N), CHIPS, 0, 0, tiled=True).reshape(ROWS * N, N)
    far = lax.ppermute(near, "c", swap)
    rows, right = apply_near(apply_meta, near, weight_grad)
    return apply_far(apply_meta, near, far, weight_grad, rows, right)


def solution(mesh):
    fine = Mesh(mesh.devices.reshape(2, 4, 4, 4, 2), ALL)
    row, col = ("zh", "x"), ("zl", "y", "c")
    placed = (P(ALL, None), P(ALL, None), P(row, col), P(ALL, None, None), P(), P())
    return jax.shard_map(
        on_device,
        mesh=fine,
        in_specs=placed,
        out_specs=(P(row, col), P(ALL, None, None)),
        check_vma=False,
    )
```

```python
import functools

import jax
import jax.numpy as jnp
import numpy as np
from jax import lax
from jax.experimental import pallas as pl
from jax.experimental.pallas import tpu as pltpu
from jax.sharding import Mesh
from jax.sharding import PartitionSpec as P

D = 5120
H = 8192
N = 128
ITERS = 6
TOKENS = 65536
NA = D // N
NB = NA + H // N
SLOTS = 256

ema_decay = 0.8

HALF = 26
TILES = HALF + 1
ALL = ("zh", "x", "zl", "y", "c")
PLANE = ("x", "y")
DEPTH = ("zh", "zl")
CHIPS = ("x", "y", "zh", "zl")
ROWS = 6


def pair_home(block):
    group, at = block // 10, (block % 10) // 2
    col = (block - NA) // 2
    last = at == 2
    high = at > 2
    a_half = jnp.where(last, group % 2, jnp.where(high, at - 3, at))
    a_place = jnp.where(last, 8 + group // 2, jnp.where(high, group + 4, group))
    is_a = block < NA
    return jnp.where(is_a, a_half, col % 2), jnp.where(is_a, a_place, 10 + col // 2)


def pair_column(place, half):
    if place < 8:
        return 0, 5 * (place % 4) + (3 if place >= 4 else 0) + half
    if place < 10:
        return 0, 5 * (half + 2 * (place - 8)) + 2
    return 1, 2 * (place - 10) + half


def lower_mask():
    r = lax.broadcasted_iota(jnp.int32, (N, N), 0)
    c = lax.broadcasted_iota(jnp.int32, (N, N), 1)
    return r, c


SCALE = (1.0 - ema_decay) / TOKENS


def gram(x):
    return lax.dot_general(x, x, (((0,), (0,)), ((), ())), preferred_element_type=jnp.float32)


GROUPS = (12, 14)
META = 5


def wanted_slots():
    at = lax.broadcasted_iota(jnp.int32, (ROWS * N, N), 0)
    chip = (at * 10923) >> 16
    kind = at - ROWS * chip
    x, y, z_hi, z_lo = chip >> 5, (chip >> 3) & 3, (chip >> 2) & 1, chip & 3
    slot = (z_hi * 4 + x) * 32 + (z_lo * 4 + y) * 2 + kind - 4
    return jnp.where(kind < 4, -1, slot)


def fixed_picks():
    x, y, zh, zl = np.unravel_index(np.arange(N), (4, 4, 2, 4))
    row, pair_col = zh * 4 + x, zl * 4 + y
    none = np.full(N, 99)
    places = [row // 2 + 4 * (row % 2), 8 + row // 4, 10 + pair_col, np.full(N, HALF), none, none]
    wanted = np.arange(96) % 32
    base = np.stack(places, axis=1).reshape(ROWS * N, 1) == wanted
    homes = np.zeros((2, N, 96), bool)
    for half in range(2):
        for place in range(HALF):
            which, pair = pair_column(place, half)
            first = (NA if which else 0) + 2 * pair
            homes[half, first : first + 2] = wanted == place
    return jnp.asarray(base, jnp.bfloat16), jnp.asarray(homes, jnp.bfloat16)


def partial_kernel(core_of, me_of, own, *refs):
    if own:
        acts, outgrads, prev_hbm, owner_hbm, owner_row, damping, base, homes = refs[:8]
        out, picks, meta, buf, prev, owner, rows, sems, small_sems = refs[8:]
    else:
        acts, outgrads, prev_hbm, owner_hbm, out_hbm, buf, prev, owner, rows, sems, small_sems, out, out_sems = refs
    core, me = core_of(), me_of()
    half = core if own else 1 - core
    small = [
        pltpu.make_async_copy(owner_hbm, owner, small_sems.at[0]),
        pltpu.make_async_copy(prev_hbm, prev, small_sems.at[1]),
    ]
    small[0].start()
    copies = []
    for place in range(HALF):
        which, pair = pair_column(place, half)
        off = pl.multiple_of(pair * (2 * N), 2 * N)
        src = (outgrads if which else acts).at[:, pl.ds(off, 2 * N)]
        copies.append(pltpu.make_async_copy(src, buf.at[place], sems.at[place]))
        copies[-1].start()
    small[1].start()
    r, c = lower_mask()
    rows[...] = jnp.zeros((N, N), jnp.float32)

    small[0].wait()
    block = jnp.int32(0)
    for i in range(NB):
        block = jnp.where(owner[i] == me, i + 1, block)
    slot = jnp.maximum(block - 1, 0)
    slot_half, slot_place = pair_home(slot)
    second_of = slot % 2

    if own:
        for i, one in enumerate([block, slot_half, slot_place, second_of]):
            meta[i] = jnp.int32(one).astype(jnp.float32)
        meta[META - 1] = damping[0]
        matches = (wanted_slots() == owner_row[0:1, :]).astype(jnp.float32).astype(jnp.bfloat16)
        found = jnp.dot(matches, homes[core], preferred_element_type=jnp.float32)
        picks[...] = (base[...].astype(jnp.float32) + found).astype(jnp.bfloat16)

    done, sent = 0, []
    for number, count in enumerate(GROUPS):
        begin, end = done, done + count
        done = end
        for place in range(begin, end):
            copies[place].wait()
        for place in range(begin, end):
            first = gram(buf[place, :, :N])
            second = gram(buf[place, :, N:])
            packed = jnp.where(r <= c, first, second) * SCALE
            out[:, place] = packed.reshape(16, 8, N)
            line = jnp.sum(jnp.where(r == c, second, 0.0), axis=0, keepdims=True)
            rows[pl.ds(32 * half + place, 1), :] = line * SCALE
        if number == 0:
            small[1].wait()

        @pl.when((block > 0) & (slot_half == half) & (slot_place >= begin) & (slot_place < end))
        def _():
            mine = jnp.where((r > c) == (second_of == 1), prev[0] * ema_decay, 0.0)
            out[:, slot_place] += mine.reshape(16, 8, N)

        at = pl.ds(begin, count)
        if end == HALF:

            @pl.when((block > 0) & (slot_half == half) & (second_of == 1))
            def _():
                line = jnp.sum(jnp.where(r == c, prev[0], 0.0), axis=0, keepdims=True)
                rows[pl.ds(32 * half + slot_place, 1), :] += line * ema_decay

            out[:, HALF] = rows[...].T.reshape(16, 8, N)
            at = pl.ds(begin, count + 1)
        if not own:
            sent.append(pltpu.make_async_copy(out.at[:, at], out_hbm.at[:, at], out_sems.at[number]))
            sent[-1].start()
    for copy in sent:
        copy.wait()


def partials(acts, outgrads, prev, owner, core_of, me_of, damping=None):
    own = damping is not None
    hbm, vmem = pl.BlockSpec(memory_space=pltpu.HBM), pl.BlockSpec(memory_space=pltpu.VMEM)
    smem = pl.BlockSpec(memory_space=pltpu.SMEM)
    shape = jax.ShapeDtypeStruct((16, TILES, 8, N), jnp.float32)
    picks_shape = jax.ShapeDtypeStruct((ROWS * N, 96), jnp.bfloat16)
    meta_shape = jax.ShapeDtypeStruct((META,), jnp.float32)
    scratch = [
        pltpu.VMEM((HALF, 256, 2 * N), jnp.bfloat16),
        pltpu.VMEM((1, N, N), jnp.float32),
        pltpu.SMEM((SLOTS,), jnp.int32),
        pltpu.VMEM((N, N), jnp.float32),
        pltpu.SemaphoreType.DMA((HALF,)),
        pltpu.SemaphoreType.DMA((2,)),
    ]
    if not own:
        scratch += [
            pltpu.VMEM((16, TILES, 8, N), jnp.float32),
            pltpu.SemaphoreType.DMA((len(GROUPS),)),
        ]
    return pl.pallas_call(
        functools.partial(partial_kernel, core_of, me_of, own),
        out_shape=(shape, picks_shape, meta_shape) if own else shape,
        in_specs=[hbm] * 4 + ([vmem, smem, vmem, vmem] if own else []),
        out_specs=(vmem, vmem, smem) if own else hbm,
        scratch_shapes=scratch,
        compiler_params=pltpu.CompilerParams(vmem_limit_bytes=(50 if own else 61) * 2**20),
        name="own_half" if own else "other_half",
    )(*((acts, outgrads, prev, owner) + ((owner.reshape(2, N), damping) + fixed_picks() if own else ())))


def add_kernel(a, b, out):
    out[...] = a[...] + b[...]


def add_cores(own, received):
    vmem = pl.BlockSpec(memory_space=pltpu.VMEM)
    return pl.pallas_call(
        add_kernel,
        out_shape=jax.ShapeDtypeStruct(own.shape, jnp.float32),
        in_specs=[vmem, vmem],
        out_specs=vmem,
        compiler_params=pltpu.CompilerParams(vmem_limit_bytes=16 * 2**20),
        name="add_cores",
    )(own, received)


def plane_kernel(got, out, total):
    for tile in range(TILES):
        parts = [got[s, pl.ds(8 * tile, 8), :] for s in range(16)]
        while len(parts) > 1:
            parts = [a + b for a, b in zip(parts[::2], parts[1::2])]
        total[pl.ds(8 * tile, 8), :] = parts[0]
    total[pl.ds(8 * TILES, 40), :] = jnp.zeros((40, N), jnp.float32)
    for z in range(8):
        out[z] = total[pl.ds(z, 32, stride=8), :]


def plane_sum(got):
    return pl.pallas_call(
        plane_kernel,
        out_shape=jax.ShapeDtypeStruct((8, 32, N), jnp.float32),
        in_specs=[pl.BlockSpec(memory_space=pltpu.VMEM)],
        out_specs=pl.BlockSpec(memory_space=pltpu.VMEM),
        scratch_shapes=[pltpu.VMEM((256, N), jnp.float32)],
        compiler_params=pltpu.CompilerParams(vmem_limit_bytes=40 * 2**20),
        name="plane_sum",
    )(got)


def thirds(x):
    high = x.astype(jnp.bfloat16)
    rest = x - high.astype(jnp.float32)
    mid = rest.astype(jnp.bfloat16)
    low = (rest - mid.astype(jnp.float32)).astype(jnp.bfloat16)
    return high, mid, low


def spread_kernel(got, picks, out):
    total = got[0]
    for z in range(1, 8):
        total = total + got[z]
    stacked = jnp.concatenate(thirds(total), axis=0)
    out[...] = jnp.dot(picks[...], stacked, preferred_element_type=jnp.float32)


def spread_rows(got, picks):
    return pl.pallas_call(
        spread_kernel,
        out_shape=jax.ShapeDtypeStruct((ROWS * N, N), jnp.float32),
        in_specs=[pl.BlockSpec(memory_space=pltpu.VMEM)] * 2,
        out_specs=pl.BlockSpec(memory_space=pltpu.VMEM),
        compiler_params=pltpu.CompilerParams(vmem_limit_bytes=40 * 2**20),
        name="spread_rows",
    )(got, picks)


def halves(x):
    high = x.astype(jnp.bfloat16)
    return high, (x - high.astype(jnp.float32)).astype(jnp.bfloat16)


def left_form(a):
    return jnp.concatenate(halves(a), axis=1)


def right_form(b):
    b1, b2 = halves(b)
    return jnp.concatenate([jnp.concatenate([b1, b2], axis=1), jnp.concatenate([b2, b1], axis=1)], axis=0)


def times(left, right):
    four = jnp.dot(left, right, preferred_element_type=jnp.float32)
    return four[:, :N] + four[:, N:]


def mul(left, b):
    return times(left, right_form(b))


def correction(e):
    e1 = e.astype(jnp.bfloat16)
    low = e - e1.astype(jnp.float32)
    e3 = (low - low.astype(jnp.bfloat16).astype(jnp.float32)).astype(jnp.bfloat16)
    return jnp.dot(
        jnp.concatenate([e1, e3], axis=1), jnp.concatenate([e3, e1], axis=0), preferred_element_type=jnp.float32
    )


def square(e):
    return mul(left_form(e), e) + correction(e)


def unpacked(packed, second, diags, lane):
    r, c = lower_mask()
    lower, on = r > c, r == c
    flipped = packed.T
    if isinstance(second, int) and second == 0:
        return jnp.where(lower, flipped, packed)
    column = jnp.sum(jnp.where(c == lane, diags, 0.0), axis=1, keepdims=True)
    if isinstance(second, int):
        return jnp.where(on, column, jnp.where(lower, packed, flipped))
    straight = jnp.where(lower, second, 1 - second) == 1
    return jnp.where(on & (second == 1), column, jnp.where(straight, packed, flipped))


def inverses(blocks, damping):
    r, c = lower_mask()
    eye = jnp.where(r == c, 1.0, 0.0)
    rest, approx = [], []
    for one in blocks:
        one = one + damping * eye
        bound = jnp.max(jnp.sum(jnp.abs(one), axis=0, keepdims=True), axis=1, keepdims=True)
        start = 1.0 / bound
        rest.append(eye - one * start)
        approx.append((eye + rest[-1]) * start)
    rest = [square(e) for e in rest]
    for step in range(1, ITERS):
        right = [right_form(e) for e in rest]
        if step == ITERS - 1:
            return [x + times(left_form(x), f) for x, f in zip(approx, right)]
        stacked = [
            times(jnp.concatenate([left_form(e), left_form(x)], axis=0), f)
            for e, x, f in zip(rest, approx, right)
        ]
        approx = [x + both[N:] for x, both in zip(approx, stacked)]
        if step == 1:
            rest = [both[:N] + correction(e) for e, both in zip(rest, stacked)]
        else:
            rest = [both[:N] for both in stacked]


def both_sides(left, w, right):
    left = left_form(left)
    parts = []
    for j in range(2):
        product = mul(left, w[:, j * N : (j + 1) * N])
        parts.append(times(left_form(product), right[j]))
    return jnp.concatenate(parts, axis=1)


def group_rows(index, odd_row):
    place = 4 * (1 - odd_row) if isinstance(index, str) else index + odd_row
    return pl.ds(pl.multiple_of(place * N, N), N)


def number(meta, i):
    return meta[i].astype(jnp.int32)


def near_kernel(places, meta_hbm, own, weight, rows_out, right_out, meta, meta_sem):
    scalars = pltpu.make_async_copy(meta_hbm, meta, meta_sem.at[0])
    scalars.start()
    core, row, col = [place() for place in places]
    group, odd_row = row // 2, row % 2

    def fetch(k):
        return own[pl.ds(k, N, stride=ROWS), :]

    diags, first, last = fetch(3), fetch(0), fetch(2)
    lane = 32 * core + group + 4 * odd_row
    blocks = [unpacked(first, second, diags, lane) for second in range(2)]
    blocks += [unpacked(last, second, diags, 32 * core + 10 + col // 2) for second in range(2)]
    scalars.wait()
    approx = inverses(blocks, meta[4])
    right = [right_form(one) for one in approx[2:]]
    for i in range(2):
        rows_out[pl.ds(i * N, N), :] = both_sides(approx[i], weight[group_rows(2 * core + i, odd_row), :], right)
        right_out[i] = right[i]


def far_kernel(places, meta_hbm, own, other, weight, rows_in, right_in, out_hbm, updated_hbm, *scratch):
    out, updated, meta, meta_sem, sems = scratch
    scalars = pltpu.make_async_copy(meta_hbm, meta, meta_sem.at[0])
    scalars.start()
    core, row, _ = [place() for place in places]
    group, odd_row = row // 2, row % 2
    fifth_half = group % 2
    sent = []

    def send(src, dst):
        sent.append(pltpu.make_async_copy(src, dst, sems.at[len(sent)]))
        sent[-1].start()

    for i in range(2):
        send(rows_in.at[pl.ds(i * N, N), :], out_hbm.at[group_rows(2 * core + i, odd_row), :])

    def fetch(ref, k):
        return ref[pl.ds(k, N, stride=ROWS), :]

    diags = fetch(own, 3) + fetch(other, 3)
    first = fetch(other, 0)
    fifth = jnp.where(fifth_half == core, fetch(own, 1), fetch(other, 1))
    lane = 32 * (1 - core) + group + 4 * odd_row
    blocks = [unpacked(first, second, diags, lane) for second in range(2)]
    blocks.append(unpacked(fifth, odd_row, diags, 32 * fifth_half + 8 + group // 2))
    scalars.wait()
    block, slot_half, slot_place, slot_second = [number(meta, i) for i in range(4)]
    mine = jnp.where(slot_half == core, fetch(own, 4 + core), fetch(other, 4 + core))
    fresh = unpacked(mine, slot_second, diags, 32 * slot_half + slot_place)
    updated[0] = jnp.where(block > 0, fresh, 0.0)
    send(updated, updated_hbm)

    approx = inverses(blocks, meta[4])
    right = [right_in[0], right_in[1]]
    for i in range(3):
        at = group_rows("fifth" if i == 2 else 2 * (1 - core) + i, odd_row)
        out[pl.ds(i * N, N), :] = both_sides(approx[i], weight[at, :], right)
        send(out.at[pl.ds(i * N, N), :], out_hbm.at[at, :])
    for copy in sent:
        copy.wait()


def apply_near(places, meta, own, weight):
    vmem, hbm = pl.BlockSpec(memory_space=pltpu.VMEM), pl.BlockSpec(memory_space=pltpu.HBM)
    return pl.pallas_call(
        functools.partial(near_kernel, places),
        out_shape=(
            jax.ShapeDtypeStruct((2 * N, 2 * N), jnp.float32),
            jax.ShapeDtypeStruct((2, 2 * N, 2 * N), jnp.bfloat16),
        ),
        in_specs=[hbm, vmem, vmem],
        out_specs=(vmem, vmem),
        scratch_shapes=[pltpu.SMEM((META,), jnp.float32), pltpu.SemaphoreType.DMA((1,))],
        compiler_params=pltpu.CompilerParams(vmem_limit_bytes=40 * 2**20),
        name="apply_near",
    )(meta, own, weight)


def apply_far(places, meta, own, other, weight, rows, right):
    vmem, hbm = pl.BlockSpec(memory_space=pltpu.VMEM), pl.BlockSpec(memory_space=pltpu.HBM)
    return pl.pallas_call(
        functools.partial(far_kernel, places),
        out_shape=(
            jax.ShapeDtypeStruct(weight.shape, jnp.float32),
            jax.ShapeDtypeStruct((1, N, N), jnp.float32),
        ),
        in_specs=[hbm] + [vmem] * 5,
        out_specs=(hbm, hbm),
        scratch_shapes=[
            pltpu.VMEM((3 * N, 2 * N), jnp.float32),
            pltpu.VMEM((1, N, N), jnp.float32),
            pltpu.SMEM((META,), jnp.float32),
            pltpu.SemaphoreType.DMA((1,)),
            pltpu.SemaphoreType.DMA((6,)),
        ],
        compiler_params=pltpu.CompilerParams(vmem_limit_bytes=40 * 2**20),
        name="apply_far",
    )(meta, own, other, weight, rows, right)


def on_device(acts, outgrads, weight_grad, prev_factor, damping, owner):
    core_of = lambda: lax.axis_index("c").astype(jnp.int32)
    row_of = lambda: lax.axis_index(("zh", "x")).astype(jnp.int32)
    col_of = lambda: lax.axis_index(("zl", "y", "c")).astype(jnp.int32)
    me_of = lambda: row_of() * 32 + col_of()

    places = (core_of, row_of, col_of)
    swap = [(0, 1), (1, 0)]
    other = partials(acts, outgrads, prev_factor, owner, core_of, me_of)
    received = lax.ppermute(other, "c", swap)
    own, picks, apply_meta = partials(acts, outgrads, prev_factor, owner, core_of, me_of, damping.reshape(1))
    chip = add_cores(own, received)

    got = lax.all_to_all(chip.reshape(16, 8 * TILES, N), PLANE, 0, 0, tiled=True)
    by_depth = plane_sum(got)
    got = lax.all_to_all(by_depth, DEPTH, 0, 0, tiled=True)
    sent = spread_rows(got, picks)
    near = lax.all_to_all(sent.reshape(N, ROWS, 1, N), CHIPS, 0, 0, tiled=True).reshape(ROWS * N, N)
    far = lax.ppermute(near, "c", swap)
    rows, right = apply_near(places, apply_meta, near, weight_grad)
    return apply_far(places, apply_meta, near, far, weight_grad, rows, right)


def solution(mesh):
    fine = Mesh(mesh.devices.reshape(2, 4, 4, 4, 2), ALL)
    row, col = ("zh", "x"), ("zl", "y", "c")
    placed = (P(ALL, None), P(ALL, None), P(row, col), P(ALL, None, None), P(), P())
    return jax.shard_map(
        on_device,
        mesh=fine,
        in_specs=placed,
        out_specs=(P(row, col), P(ALL, None, None)),
        check_vma=False,
    )
```

```python
import functools

import jax
import jax.numpy as jnp
import numpy as np
from jax import lax
from jax.experimental import pallas as pl
from jax.experimental.pallas import tpu as pltpu
from jax.sharding import Mesh
from jax.sharding import PartitionSpec as P

D = 5120
H = 8192
N = 128
ITERS = 6
TOKENS = 65536
NA = D // N
NB = NA + H // N
SLOTS = 256

ema_decay = 0.8

HALF = 26
TILES = HALF + 1
ALL = ("zh", "x", "zl", "y", "c")
PLANE = ("x", "y")
DEPTH = ("zh", "zl")
CHIPS = ("x", "y", "zh", "zl")
ROWS = 6


def pair_home(block):
    group, at = block // 10, (block % 10) // 2
    col = (block - NA) // 2
    last = at == 2
    high = at > 2
    a_half = jnp.where(last, group % 2, jnp.where(high, at - 3, at))
    a_place = jnp.where(last, 8 + group // 2, jnp.where(high, group + 4, group))
    is_a = block < NA
    return jnp.where(is_a, a_half, col % 2), jnp.where(is_a, a_place, 10 + col // 2)


def pair_column(place, half):
    if place < 8:
        return 0, 5 * (place % 4) + (3 if place >= 4 else 0) + half
    if place < 10:
        return 0, 5 * (half + 2 * (place - 8)) + 2
    return 1, 2 * (place - 10) + half


def lower_mask():
    r = lax.broadcasted_iota(jnp.int32, (N, N), 0)
    c = lax.broadcasted_iota(jnp.int32, (N, N), 1)
    return r, c


SCALE = (1.0 - ema_decay) / TOKENS


def gram(x):
    return lax.dot_general(x, x, (((0,), (0,)), ((), ())), preferred_element_type=jnp.float32)


GROUPS = (12, 14)


def wanted_slots():
    at = lax.broadcasted_iota(jnp.int32, (ROWS * N, N), 0)
    chip = (at * 10923) >> 16
    kind = at - ROWS * chip
    x, y, z_hi, z_lo = chip >> 5, (chip >> 3) & 3, (chip >> 2) & 1, chip & 3
    slot = (z_hi * 4 + x) * 32 + (z_lo * 4 + y) * 2 + kind - 4
    return jnp.where(kind < 4, -1, slot)


def fixed_picks():
    x, y, zh, zl = np.unravel_index(np.arange(N), (4, 4, 2, 4))
    row, pair_col = zh * 4 + x, zl * 4 + y
    none = np.full(N, 99)
    places = [row // 2 + 4 * (row % 2), 8 + row // 4, 10 + pair_col, np.full(N, HALF), none, none]
    wanted = np.arange(96) % 32
    base = np.stack(places, axis=1).reshape(ROWS * N, 1) == wanted
    homes = np.zeros((2, N, 96), bool)
    for half in range(2):
        for place in range(HALF):
            which, pair = pair_column(place, half)
            first = (NA if which else 0) + 2 * pair
            homes[half, first : first + 2] = wanted == place
    return jnp.asarray(base, jnp.bfloat16), jnp.asarray(homes, jnp.bfloat16)


def partial_kernel(core_of, me_of, own, *refs):
    if own:
        acts, outgrads, prev_hbm, owner_hbm, owner_row, damping_hbm, base, homes = refs[:8]
        out, picks, meta, buf, prev, owner, rows, sems, small_sems, damping = refs[8:]
    else:
        acts, outgrads, prev_hbm, owner_hbm, out_hbm, buf, prev, owner, rows, sems, small_sems, out, out_sems = refs
    core, me = core_of(), me_of()
    half = core if own else 1 - core
    small = [
        pltpu.make_async_copy(owner_hbm, owner, small_sems.at[0]),
        pltpu.make_async_copy(prev_hbm, prev, small_sems.at[1]),
    ]
    small[0].start()
    if own:
        small.append(pltpu.make_async_copy(damping_hbm, damping, small_sems.at[2]))
        small[2].start()
    copies = []
    for place in range(HALF):
        which, pair = pair_column(place, half)
        off = pl.multiple_of(pair * (2 * N), 2 * N)
        src = (outgrads if which else acts).at[:, pl.ds(off, 2 * N)]
        copies.append(pltpu.make_async_copy(src, buf.at[place], sems.at[place]))
        copies[-1].start()
    small[1].start()
    r, c = lower_mask()
    rows[...] = jnp.zeros((N, N), jnp.float32)

    small[0].wait()
    block = jnp.int32(0)
    for i in range(NB):
        block = jnp.where(owner[i] == me, i + 1, block)
    slot = jnp.maximum(block - 1, 0)
    slot_half, slot_place = pair_home(slot)
    second_of = slot % 2

    if own:
        small[2].wait()
        lane = lax.broadcasted_iota(jnp.int32, (8, N), 1)
        scalars = jnp.full((8, N), damping[0])
        for i, one in enumerate([block, slot_half, slot_place, second_of]):
            scalars = jnp.where(lane == i, jnp.int32(one).astype(jnp.float32), scalars)
        meta[...] = scalars
        matches = (wanted_slots() == owner_row[0:1, :]).astype(jnp.float32).astype(jnp.bfloat16)
        found = jnp.dot(matches, homes[core], preferred_element_type=jnp.float32)
        picks[...] = (base[...].astype(jnp.float32) + found).astype(jnp.bfloat16)

    done, sent = 0, []
    for number, count in enumerate(GROUPS):
        begin, end = done, done + count
        done = end
        for place in range(begin, end):
            copies[place].wait()
        for place in range(begin, end):
            first = gram(buf[place, :, :N])
            second = gram(buf[place, :, N:])
            packed = jnp.where(r <= c, first, second) * SCALE
            out[:, place] = packed.reshape(16, 8, N)
            line = jnp.sum(jnp.where(r == c, second, 0.0), axis=0, keepdims=True)
            rows[pl.ds(32 * half + place, 1), :] = line * SCALE
        if number == 0:
            small[1].wait()

        @pl.when((block > 0) & (slot_half == half) & (slot_place >= begin) & (slot_place < end))
        def _():
            mine = jnp.where((r > c) == (second_of == 1), prev[0] * ema_decay, 0.0)
            out[:, slot_place] += mine.reshape(16, 8, N)

        at = pl.ds(begin, count)
        if end == HALF:

            @pl.when((block > 0) & (slot_half == half) & (second_of == 1))
            def _():
                line = jnp.sum(jnp.where(r == c, prev[0], 0.0), axis=0, keepdims=True)
                rows[pl.ds(32 * half + slot_place, 1), :] += line * ema_decay

            out[:, HALF] = rows[...].T.reshape(16, 8, N)
            at = pl.ds(begin, count + 1)
        if not own:
            sent.append(pltpu.make_async_copy(out.at[:, at], out_hbm.at[:, at], out_sems.at[number]))
            sent[-1].start()
    for copy in sent:
        copy.wait()


def partials(acts, outgrads, prev, owner, core_of, me_of, damping=None):
    own = damping is not None
    hbm, vmem = pl.BlockSpec(memory_space=pltpu.HBM), pl.BlockSpec(memory_space=pltpu.VMEM)
    shape = jax.ShapeDtypeStruct((16, TILES, 8, N), jnp.float32)
    picks_shape = jax.ShapeDtypeStruct((ROWS * N, 96), jnp.bfloat16)
    meta_shape = jax.ShapeDtypeStruct((8, N), jnp.float32)
    scratch = [
        pltpu.VMEM((HALF, 256, 2 * N), jnp.bfloat16),
        pltpu.VMEM((1, N, N), jnp.float32),
        pltpu.SMEM((SLOTS,), jnp.int32),
        pltpu.VMEM((N, N), jnp.float32),
        pltpu.SemaphoreType.DMA((HALF,)),
        pltpu.SemaphoreType.DMA((3,)),
    ]
    if own:
        scratch += [pltpu.SMEM((1,), jnp.float32)]
    else:
        scratch += [
            pltpu.VMEM((16, TILES, 8, N), jnp.float32),
            pltpu.SemaphoreType.DMA((len(GROUPS),)),
        ]
    return pl.pallas_call(
        functools.partial(partial_kernel, core_of, me_of, own),
        out_shape=(shape, picks_shape, meta_shape) if own else shape,
        in_specs=[hbm] * 4 + ([vmem, hbm, vmem, vmem] if own else []),
        out_specs=(vmem, vmem, vmem) if own else hbm,
        scratch_shapes=scratch,
        compiler_params=pltpu.CompilerParams(vmem_limit_bytes=(50 if own else 61) * 2**20),
        name="own_half" if own else "other_half",
    )(*((acts, outgrads, prev, owner) + ((owner.reshape(2, N), damping) + fixed_picks() if own else ())))


def add_kernel(a, b, out):
    out[...] = a[...] + b[...]


def add_cores(own, received):
    vmem = pl.BlockSpec(memory_space=pltpu.VMEM)
    return pl.pallas_call(
        add_kernel,
        out_shape=jax.ShapeDtypeStruct(own.shape, jnp.float32),
        in_specs=[vmem, vmem],
        out_specs=vmem,
        compiler_params=pltpu.CompilerParams(vmem_limit_bytes=16 * 2**20),
        name="add_cores",
    )(own, received)


def plane_kernel(got, out, total):
    for tile in range(TILES):
        parts = [got[s, pl.ds(8 * tile, 8), :] for s in range(16)]
        while len(parts) > 1:
            parts = [a + b for a, b in zip(parts[::2], parts[1::2])]
        total[pl.ds(8 * tile, 8), :] = parts[0]
    total[pl.ds(8 * TILES, 40), :] = jnp.zeros((40, N), jnp.float32)
    for z in range(8):
        out[z] = total[pl.ds(z, 32, stride=8), :]


def plane_sum(got):
    return pl.pallas_call(
        plane_kernel,
        out_shape=jax.ShapeDtypeStruct((8, 32, N), jnp.float32),
        in_specs=[pl.BlockSpec(memory_space=pltpu.VMEM)],
        out_specs=pl.BlockSpec(memory_space=pltpu.VMEM),
        scratch_shapes=[pltpu.VMEM((256, N), jnp.float32)],
        compiler_params=pltpu.CompilerParams(vmem_limit_bytes=40 * 2**20),
        name="plane_sum",
    )(got)


def thirds(x):
    high = x.astype(jnp.bfloat16)
    rest = x - high.astype(jnp.float32)
    mid = rest.astype(jnp.bfloat16)
    low = (rest - mid.astype(jnp.float32)).astype(jnp.bfloat16)
    return high, mid, low


def spread_kernel(got, picks, out):
    total = got[0]
    for z in range(1, 8):
        total = total + got[z]
    stacked = jnp.concatenate(thirds(total), axis=0)
    out[...] = jnp.dot(picks[...], stacked, preferred_element_type=jnp.float32)


def spread_rows(got, picks):
    return pl.pallas_call(
        spread_kernel,
        out_shape=jax.ShapeDtypeStruct((ROWS * N, N), jnp.float32),
        in_specs=[pl.BlockSpec(memory_space=pltpu.VMEM)] * 2,
        out_specs=pl.BlockSpec(memory_space=pltpu.VMEM),
        compiler_params=pltpu.CompilerParams(vmem_limit_bytes=40 * 2**20),
        name="spread_rows",
    )(got, picks)


def halves(x):
    high = x.astype(jnp.bfloat16)
    return high, (x - high.astype(jnp.float32)).astype(jnp.bfloat16)


def left_form(a):
    return jnp.concatenate(halves(a), axis=1)


def right_form(b):
    b1, b2 = halves(b)
    return jnp.concatenate([jnp.concatenate([b1, b2], axis=1), jnp.concatenate([b2, b1], axis=1)], axis=0)


def times(left, right):
    four = jnp.dot(left, right, preferred_element_type=jnp.float32)
    return four[:, :N] + four[:, N:]


def mul(left, b):
    return times(left, right_form(b))


def correction(e):
    e1 = e.astype(jnp.bfloat16)
    low = e - e1.astype(jnp.float32)
    e3 = (low - low.astype(jnp.bfloat16).astype(jnp.float32)).astype(jnp.bfloat16)
    return jnp.dot(
        jnp.concatenate([e1, e3], axis=1), jnp.concatenate([e3, e1], axis=0), preferred_element_type=jnp.float32
    )


def square(e):
    return mul(left_form(e), e) + correction(e)


def unpacked(packed, second, diags, lane):
    r, c = lower_mask()
    lower, on = r > c, r == c
    flipped = packed.T
    if isinstance(second, int) and second == 0:
        return jnp.where(lower, flipped, packed)
    column = jnp.sum(jnp.where(c == lane, diags, 0.0), axis=1, keepdims=True)
    if isinstance(second, int):
        return jnp.where(on, column, jnp.where(lower, packed, flipped))
    straight = jnp.where(lower, second, 1 - second) == 1
    return jnp.where(on & (second == 1), column, jnp.where(straight, packed, flipped))


def inverses(blocks, damping):
    r, c = lower_mask()
    eye = jnp.where(r == c, 1.0, 0.0)
    rest, approx = [], []
    for one in blocks:
        one = one + damping * eye
        bound = jnp.max(jnp.sum(jnp.abs(one), axis=0, keepdims=True), axis=1, keepdims=True)
        start = 1.0 / bound
        rest.append(eye - one * start)
        approx.append((eye + rest[-1]) * start)
    rest = [square(e) for e in rest]
    for step in range(1, ITERS):
        right = [right_form(e) for e in rest]
        if step == ITERS - 1:
            return [x + times(left_form(x), f) for x, f in zip(approx, right)]
        stacked = [
            times(jnp.concatenate([left_form(e), left_form(x)], axis=0), f)
            for e, x, f in zip(rest, approx, right)
        ]
        approx = [x + both[N:] for x, both in zip(approx, stacked)]
        if step == 1:
            rest = [both[:N] + correction(e) for e, both in zip(rest, stacked)]
        else:
            rest = [both[:N] for both in stacked]


def both_sides(left, w, right):
    left = left_form(left)
    parts = []
    for j in range(2):
        product = mul(left, w[:, j * N : (j + 1) * N])
        parts.append(times(left_form(product), right[j]))
    return jnp.concatenate(parts, axis=1)


def group_rows(index, odd_row):
    place = 4 * (1 - odd_row) if isinstance(index, str) else index + odd_row
    return pl.ds(pl.multiple_of(place * N, N), N)


def number(meta, i):
    return meta[0, i].astype(jnp.int32)


def near_kernel(places, meta_hbm, own, weight, rows_out, right_out, meta, meta_sem):
    scalars = pltpu.make_async_copy(meta_hbm.at[pl.ds(0, 1)], meta, meta_sem.at[0])
    scalars.start()
    core, row, col = [place() for place in places]
    group, odd_row = row // 2, row % 2

    def fetch(k):
        return own[pl.ds(k, N, stride=ROWS), :]

    diags, first, last = fetch(3), fetch(0), fetch(2)
    lane = 32 * core + group + 4 * odd_row
    blocks = [unpacked(first, second, diags, lane) for second in range(2)]
    blocks += [unpacked(last, second, diags, 32 * core + 10 + col // 2) for second in range(2)]
    scalars.wait()
    approx = inverses(blocks, meta[0, 4])
    right = [right_form(one) for one in approx[2:]]
    for i in range(2):
        rows_out[pl.ds(i * N, N), :] = both_sides(approx[i], weight[group_rows(2 * core + i, odd_row), :], right)
        right_out[i] = right[i]


def far_kernel(places, meta_hbm, own, other, weight, rows_in, right_in, out_hbm, updated_hbm, *scratch):
    out, updated, meta, meta_sem, sems = scratch
    scalars = pltpu.make_async_copy(meta_hbm.at[pl.ds(0, 1)], meta, meta_sem.at[0])
    scalars.start()
    core, row, _ = [place() for place in places]
    group, odd_row = row // 2, row % 2
    fifth_half = group % 2
    sent = []

    def send(src, dst):
        sent.append(pltpu.make_async_copy(src, dst, sems.at[len(sent)]))
        sent[-1].start()

    for i in range(2):
        send(rows_in.at[pl.ds(i * N, N), :], out_hbm.at[group_rows(2 * core + i, odd_row), :])

    def fetch(ref, k):
        return ref[pl.ds(k, N, stride=ROWS), :]

    diags = fetch(own, 3) + fetch(other, 3)
    first = fetch(other, 0)
    fifth = jnp.where(fifth_half == core, fetch(own, 1), fetch(other, 1))
    lane = 32 * (1 - core) + group + 4 * odd_row
    blocks = [unpacked(first, second, diags, lane) for second in range(2)]
    blocks.append(unpacked(fifth, odd_row, diags, 32 * fifth_half + 8 + group // 2))
    scalars.wait()
    block, slot_half, slot_place, slot_second = [number(meta, i) for i in range(4)]
    mine = jnp.where(slot_half == core, fetch(own, 4 + core), fetch(other, 4 + core))
    fresh = unpacked(mine, slot_second, diags, 32 * slot_half + slot_place)
    updated[0] = jnp.where(block > 0, fresh, 0.0)
    send(updated, updated_hbm)

    approx = inverses(blocks, meta[0, 4])
    right = [right_in[0], right_in[1]]
    for i in range(3):
        at = group_rows("fifth" if i == 2 else 2 * (1 - core) + i, odd_row)
        out[pl.ds(i * N, N), :] = both_sides(approx[i], weight[at, :], right)
        send(out.at[pl.ds(i * N, N), :], out_hbm.at[at, :])
    for copy in sent:
        copy.wait()


def apply_near(places, meta, own, weight):
    vmem, hbm = pl.BlockSpec(memory_space=pltpu.VMEM), pl.BlockSpec(memory_space=pltpu.HBM)
    return pl.pallas_call(
        functools.partial(near_kernel, places),
        out_shape=(
            jax.ShapeDtypeStruct((2 * N, 2 * N), jnp.float32),
            jax.ShapeDtypeStruct((2, 2 * N, 2 * N), jnp.bfloat16),
        ),
        in_specs=[hbm, vmem, vmem],
        out_specs=(vmem, vmem),
        scratch_shapes=[pltpu.SMEM((1, N), jnp.float32), pltpu.SemaphoreType.DMA((1,))],
        compiler_params=pltpu.CompilerParams(vmem_limit_bytes=40 * 2**20),
        name="apply_near",
    )(meta, own, weight)


def apply_far(places, meta, own, other, weight, rows, right):
    vmem, hbm = pl.BlockSpec(memory_space=pltpu.VMEM), pl.BlockSpec(memory_space=pltpu.HBM)
    return pl.pallas_call(
        functools.partial(far_kernel, places),
        out_shape=(
            jax.ShapeDtypeStruct(weight.shape, jnp.float32),
            jax.ShapeDtypeStruct((1, N, N), jnp.float32),
        ),
        in_specs=[hbm] + [vmem] * 5,
        out_specs=(hbm, hbm),
        scratch_shapes=[
            pltpu.VMEM((3 * N, 2 * N), jnp.float32),
            pltpu.VMEM((1, N, N), jnp.float32),
            pltpu.SMEM((1, N), jnp.float32),
            pltpu.SemaphoreType.DMA((1,)),
            pltpu.SemaphoreType.DMA((6,)),
        ],
        compiler_params=pltpu.CompilerParams(vmem_limit_bytes=40 * 2**20),
        name="apply_far",
    )(meta, own, other, weight, rows, right)


def on_device(acts, outgrads, weight_grad, prev_factor, damping, owner):
    core_of = lambda: lax.axis_index("c").astype(jnp.int32)
    row_of = lambda: lax.axis_index(("zh", "x")).astype(jnp.int32)
    col_of = lambda: lax.axis_index(("zl", "y", "c")).astype(jnp.int32)
    me_of = lambda: row_of() * 32 + col_of()

    places = (core_of, row_of, col_of)
    swap = [(0, 1), (1, 0)]
    other = partials(acts, outgrads, prev_factor, owner, core_of, me_of)
    received = lax.ppermute(other, "c", swap)
    own, picks, apply_meta = partials(acts, outgrads, prev_factor, owner, core_of, me_of, damping.reshape(1))
    chip = add_cores(own, received)

    got = lax.all_to_all(chip.reshape(16, 8 * TILES, N), PLANE, 0, 0, tiled=True)
    by_depth = plane_sum(got)
    got = lax.all_to_all(by_depth, DEPTH, 0, 0, tiled=True)
    sent = spread_rows(got, picks)
    near = lax.all_to_all(sent.reshape(N, ROWS, 1, N), CHIPS, 0, 0, tiled=True).reshape(ROWS * N, N)
    far = lax.ppermute(near, "c", swap)
    rows, right = apply_near(places, apply_meta, near, weight_grad)
    return apply_far(places, apply_meta, near, far, weight_grad, rows, right)


def solution(mesh):
    fine = Mesh(mesh.devices.reshape(2, 4, 4, 4, 2), ALL)
    row, col = ("zh", "x"), ("zl", "y", "c")
    placed = (P(ALL, None), P(ALL, None), P(row, col), P(ALL, None, None), P(), P())
    return jax.shard_map(
        on_device,
        mesh=fine,
        in_specs=placed,
        out_specs=(P(row, col), P(ALL, None, None)),
        check_vma=False,
    )
```

```python
import functools

import jax
import jax.numpy as jnp
import numpy as np
from jax import lax
from jax.experimental import pallas as pl
from jax.experimental.pallas import tpu as pltpu
from jax.sharding import Mesh
from jax.sharding import PartitionSpec as P

D = 5120
H = 8192
N = 128
ITERS = 6
TOKENS = 65536
NA = D // N
NB = NA + H // N
SLOTS = 256

ema_decay = 0.8

HALF = 26
TILES = HALF + 1
ALL = ("zh", "x", "zl", "y", "c")
PLANE = ("x", "y")
DEPTH = ("zh", "zl")
CHIPS = ("x", "y", "zh", "zl")
ROWS = 6


def pair_home(block):
    group, at = block // 10, (block % 10) // 2
    col = (block - NA) // 2
    last = at == 2
    high = at > 2
    a_half = jnp.where(last, group % 2, jnp.where(high, at - 3, at))
    a_place = jnp.where(last, 8 + group // 2, jnp.where(high, group + 4, group))
    is_a = block < NA
    return jnp.where(is_a, a_half, col % 2), jnp.where(is_a, a_place, 10 + col // 2)


def pair_column(place, half):
    if place < 8:
        return 0, 5 * (place % 4) + (3 if place >= 4 else 0) + half
    if place < 10:
        return 0, 5 * (half + 2 * (place - 8)) + 2
    return 1, 2 * (place - 10) + half


def lower_mask():
    r = lax.broadcasted_iota(jnp.int32, (N, N), 0)
    c = lax.broadcasted_iota(jnp.int32, (N, N), 1)
    return r, c


SCALE = (1.0 - ema_decay) / TOKENS


def gram(x):
    return lax.dot_general(x, x, (((0,), (0,)), ((), ())), preferred_element_type=jnp.float32)


GROUPS = (12, 10, 4)


def wanted_slots():
    at = lax.broadcasted_iota(jnp.int32, (ROWS * N, N), 0)
    chip = (at * 10923) >> 16
    kind = at - ROWS * chip
    x, y, z_hi, z_lo = chip >> 5, (chip >> 3) & 3, (chip >> 2) & 1, chip & 3
    slot = (z_hi * 4 + x) * 32 + (z_lo * 4 + y) * 2 + kind - 4
    return jnp.where(kind < 4, -1, slot)


def fixed_picks():
    x, y, zh, zl = np.unravel_index(np.arange(N), (4, 4, 2, 4))
    row, pair_col = zh * 4 + x, zl * 4 + y
    none = np.full(N, 99)
    places = [row // 2 + 4 * (row % 2), 8 + row // 4, 10 + pair_col, np.full(N, HALF), none, none]
    wanted = np.arange(96) % 32
    base = np.stack(places, axis=1).reshape(ROWS * N, 1) == wanted
    homes = np.zeros((2, N, 96), bool)
    for half in range(2):
        for place in range(HALF):
            which, pair = pair_column(place, half)
            first = (NA if which else 0) + 2 * pair
            homes[half, first : first + 2] = wanted == place
    return jnp.asarray(base, jnp.bfloat16), jnp.asarray(homes, jnp.bfloat16)


def partial_kernel(core_of, me_of, own, *refs):
    if own:
        acts, outgrads, prev_hbm, owner_hbm, owner_row, damping_hbm, base, homes = refs[:8]
        out, picks, meta, buf, prev, owner, rows, sems, small_sems, damping = refs[8:]
    else:
        acts, outgrads, prev_hbm, owner_hbm, out_hbm, buf, prev, owner, rows, sems, small_sems, out, out_sems = refs
    core, me = core_of(), me_of()
    half = core if own else 1 - core
    small = [
        pltpu.make_async_copy(owner_hbm, owner, small_sems.at[0]),
        pltpu.make_async_copy(prev_hbm, prev, small_sems.at[1]),
    ]
    small[0].start()
    if own:
        small.append(pltpu.make_async_copy(damping_hbm, damping, small_sems.at[2]))
        small[2].start()
    copies = []
    for place in range(HALF):
        which, pair = pair_column(place, half)
        off = pl.multiple_of(pair * (2 * N), 2 * N)
        src = (outgrads if which else acts).at[:, pl.ds(off, 2 * N)]
        copies.append(pltpu.make_async_copy(src, buf.at[place], sems.at[place]))
        copies[-1].start()
    small[1].start()
    r, c = lower_mask()
    rows[...] = jnp.zeros((N, N), jnp.float32)

    small[0].wait()
    block = jnp.int32(0)
    for i in range(NB):
        block = jnp.where(owner[i] == me, i + 1, block)
    slot = jnp.maximum(block - 1, 0)
    slot_half, slot_place = pair_home(slot)
    second_of = slot % 2

    if own:
        small[2].wait()
        lane = lax.broadcasted_iota(jnp.int32, (8, N), 1)
        scalars = jnp.full((8, N), damping[0])
        for i, one in enumerate([block, slot_half, slot_place, second_of]):
            scalars = jnp.where(lane == i, jnp.int32(one).astype(jnp.float32), scalars)
        meta[...] = scalars
        matches = (wanted_slots() == owner_row[0:1, :]).astype(jnp.float32).astype(jnp.bfloat16)
        found = jnp.dot(matches, homes[core], preferred_element_type=jnp.float32)
        picks[...] = (base[...].astype(jnp.float32) + found).astype(jnp.bfloat16)

    done, sent = 0, []
    for number, count in enumerate(GROUPS):
        begin, end = done, done + count
        done = end
        for place in range(begin, end):
            copies[place].wait()
        for place in range(begin, end):
            first = gram(buf[place, :, :N])
            second = gram(buf[place, :, N:])
            packed = jnp.where(r <= c, first, second) * SCALE
            out[:, place] = packed.reshape(16, 8, N)
            line = jnp.sum(jnp.where(r == c, second, 0.0), axis=0, keepdims=True)
            rows[pl.ds(32 * half + place, 1), :] = line * SCALE
        if number == 0:
            small[1].wait()

        @pl.when((block > 0) & (slot_half == half) & (slot_place >= begin) & (slot_place < end))
        def _():
            mine = jnp.where((r > c) == (second_of == 1), prev[0] * ema_decay, 0.0)
            out[:, slot_place] += mine.reshape(16, 8, N)

        at = pl.ds(begin, count)
        if end == HALF:

            @pl.when((block > 0) & (slot_half == half) & (second_of == 1))
            def _():
                line = jnp.sum(jnp.where(r == c, prev[0], 0.0), axis=0, keepdims=True)
                rows[pl.ds(32 * half + slot_place, 1), :] += line * ema_decay

            out[:, HALF] = rows[...].T.reshape(16, 8, N)
            at = pl.ds(begin, count + 1)
        if not own:
            sent.append(pltpu.make_async_copy(out.at[:, at], out_hbm.at[:, at], out_sems.at[number]))
            sent[-1].start()
    for copy in sent:
        copy.wait()


def partials(acts, outgrads, prev, owner, core_of, me_of, damping=None):
    own = damping is not None
    hbm, vmem = pl.BlockSpec(memory_space=pltpu.HBM), pl.BlockSpec(memory_space=pltpu.VMEM)
    shape = jax.ShapeDtypeStruct((16, TILES, 8, N), jnp.float32)
    picks_shape = jax.ShapeDtypeStruct((ROWS * N, 96), jnp.bfloat16)
    meta_shape = jax.ShapeDtypeStruct((8, N), jnp.float32)
    scratch = [
        pltpu.VMEM((HALF, 256, 2 * N), jnp.bfloat16),
        pltpu.VMEM((1, N, N), jnp.float32),
        pltpu.SMEM((SLOTS,), jnp.int32),
        pltpu.VMEM((N, N), jnp.float32),
        pltpu.SemaphoreType.DMA((HALF,)),
        pltpu.SemaphoreType.DMA((3,)),
    ]
    if own:
        scratch += [pltpu.SMEM((1,), jnp.float32)]
    else:
        scratch += [
            pltpu.VMEM((16, TILES, 8, N), jnp.float32),
            pltpu.SemaphoreType.DMA((len(GROUPS),)),
        ]
    return pl.pallas_call(
        functools.partial(partial_kernel, core_of, me_of, own),
        out_shape=(shape, picks_shape, meta_shape) if own else shape,
        in_specs=[hbm] * 4 + ([vmem, hbm, vmem, vmem] if own else []),
        out_specs=(vmem, vmem, vmem) if own else hbm,
        scratch_shapes=scratch,
        compiler_params=pltpu.CompilerParams(vmem_limit_bytes=(50 if own else 61) * 2**20),
        name="own_half" if own else "other_half",
    )(*((acts, outgrads, prev, owner) + ((owner.reshape(2, N), damping) + fixed_picks() if own else ())))


def add_kernel(a, b, out):
    out[...] = a[...] + b[...]


def add_cores(own, received):
    vmem = pl.BlockSpec(memory_space=pltpu.VMEM)
    return pl.pallas_call(
        add_kernel,
        out_shape=jax.ShapeDtypeStruct(own.shape, jnp.float32),
        in_specs=[vmem, vmem],
        out_specs=vmem,
        compiler_params=pltpu.CompilerParams(vmem_limit_bytes=16 * 2**20),
        name="add_cores",
    )(own, received)


def plane_kernel(got, out, total):
    for tile in range(TILES):
        parts = [got[s, pl.ds(8 * tile, 8), :] for s in range(16)]
        while len(parts) > 1:
            parts = [a + b for a, b in zip(parts[::2], parts[1::2])]
        total[pl.ds(8 * tile, 8), :] = parts[0]
    total[pl.ds(8 * TILES, 40), :] = jnp.zeros((40, N), jnp.float32)
    for z in range(8):
        out[z] = total[pl.ds(z, 32, stride=8), :]


def plane_sum(got):
    return pl.pallas_call(
        plane_kernel,
        out_shape=jax.ShapeDtypeStruct((8, 32, N), jnp.float32),
        in_specs=[pl.BlockSpec(memory_space=pltpu.VMEM)],
        out_specs=pl.BlockSpec(memory_space=pltpu.VMEM),
        scratch_shapes=[pltpu.VMEM((256, N), jnp.float32)],
        compiler_params=pltpu.CompilerParams(vmem_limit_bytes=40 * 2**20),
        name="plane_sum",
    )(got)


def thirds(x):
    high = x.astype(jnp.bfloat16)
    rest = x - high.astype(jnp.float32)
    mid = rest.astype(jnp.bfloat16)
    low = (rest - mid.astype(jnp.float32)).astype(jnp.bfloat16)
    return high, mid, low


def spread_kernel(got, picks, out):
    total = got[0]
    for z in range(1, 8):
        total = total + got[z]
    stacked = jnp.concatenate(thirds(total), axis=0)
    out[...] = jnp.dot(picks[...], stacked, preferred_element_type=jnp.float32)


def spread_rows(got, picks):
    return pl.pallas_call(
        spread_kernel,
        out_shape=jax.ShapeDtypeStruct((ROWS * N, N), jnp.float32),
        in_specs=[pl.BlockSpec(memory_space=pltpu.VMEM)] * 2,
        out_specs=pl.BlockSpec(memory_space=pltpu.VMEM),
        compiler_params=pltpu.CompilerParams(vmem_limit_bytes=40 * 2**20),
        name="spread_rows",
    )(got, picks)


def halves(x):
    high = x.astype(jnp.bfloat16)
    return high, (x - high.astype(jnp.float32)).astype(jnp.bfloat16)


def left_form(a):
    return jnp.concatenate(halves(a), axis=1)


def right_form(b):
    b1, b2 = halves(b)
    return jnp.concatenate([jnp.concatenate([b1, b2], axis=1), jnp.concatenate([b2, b1], axis=1)], axis=0)


def times(left, right):
    four = jnp.dot(left, right, preferred_element_type=jnp.float32)
    return four[:, :N] + four[:, N:]


def mul(left, b):
    return times(left, right_form(b))


def correction(e):
    e1 = e.astype(jnp.bfloat16)
    low = e - e1.astype(jnp.float32)
    e3 = (low - low.astype(jnp.bfloat16).astype(jnp.float32)).astype(jnp.bfloat16)
    return jnp.dot(
        jnp.concatenate([e1, e3], axis=1), jnp.concatenate([e3, e1], axis=0), preferred_element_type=jnp.float32
    )


def square(e):
    return mul(left_form(e), e) + correction(e)


def unpacked(packed, second, diags, lane):
    r, c = lower_mask()
    lower, on = r > c, r == c
    flipped = packed.T
    if isinstance(second, int) and second == 0:
        return jnp.where(lower, flipped, packed)
    column = jnp.sum(jnp.where(c == lane, diags, 0.0), axis=1, keepdims=True)
    if isinstance(second, int):
        return jnp.where(on, column, jnp.where(lower, packed, flipped))
    straight = jnp.where(lower, second, 1 - second) == 1
    return jnp.where(on & (second == 1), column, jnp.where(straight, packed, flipped))


def inverses(blocks, damping):
    r, c = lower_mask()
    eye = jnp.where(r == c, 1.0, 0.0)
    rest, approx = [], []
    for one in blocks:
        one = one + damping * eye
        bound = jnp.max(jnp.sum(jnp.abs(one), axis=0, keepdims=True), axis=1, keepdims=True)
        start = 1.0 / bound
        rest.append(eye - one * start)
        approx.append((eye + rest[-1]) * start)
    rest = [square(e) for e in rest]
    for step in range(1, ITERS):
        right = [right_form(e) for e in rest]
        if step == ITERS - 1:
            return [x + times(left_form(x), f) for x, f in zip(approx, right)]
        stacked = [
            times(jnp.concatenate([left_form(e), left_form(x)], axis=0), f)
            for e, x, f in zip(rest, approx, right)
        ]
        approx = [x + both[N:] for x, both in zip(approx, stacked)]
        if step == 1:
            rest = [both[:N] + correction(e) for e, both in zip(rest, stacked)]
        else:
            rest = [both[:N] for both in stacked]


def both_sides(left, w, right):
    left = left_form(left)
    parts = []
    for j in range(2):
        product = mul(left, w[:, j * N : (j + 1) * N])
        parts.append(times(left_form(product), right[j]))
    return jnp.concatenate(parts, axis=1)


def group_rows(index, odd_row):
    place = 4 * (1 - odd_row) if isinstance(index, str) else index + odd_row
    return pl.ds(pl.multiple_of(place * N, N), N)


def number(meta, i):
    return meta[0, i].astype(jnp.int32)


def near_kernel(places, meta_hbm, own, weight, rows_out, right_out, meta, meta_sem):
    scalars = pltpu.make_async_copy(meta_hbm.at[pl.ds(0, 1)], meta, meta_sem.at[0])
    scalars.start()
    core, row, col = [place() for place in places]
    group, odd_row = row // 2, row % 2

    def fetch(k):
        return own[pl.ds(k, N, stride=ROWS), :]

    diags, first, last = fetch(3), fetch(0), fetch(2)
    lane = 32 * core + group + 4 * odd_row
    blocks = [unpacked(first, second, diags, lane) for second in range(2)]
    blocks += [unpacked(last, second, diags, 32 * core + 10 + col // 2) for second in range(2)]
    scalars.wait()
    approx = inverses(blocks, meta[0, 4])
    right = [right_form(one) for one in approx[2:]]
    for i in range(2):
        rows_out[pl.ds(i * N, N), :] = both_sides(approx[i], weight[group_rows(2 * core + i, odd_row), :], right)
        right_out[i] = right[i]


def far_kernel(places, meta_hbm, own, other, weight, rows_in, right_in, out_hbm, updated_hbm, *scratch):
    out, updated, meta, meta_sem, sems = scratch
    scalars = pltpu.make_async_copy(meta_hbm.at[pl.ds(0, 1)], meta, meta_sem.at[0])
    scalars.start()
    core, row, _ = [place() for place in places]
    group, odd_row = row // 2, row % 2
    fifth_half = group % 2
    sent = []

    def send(src, dst):
        sent.append(pltpu.make_async_copy(src, dst, sems.at[len(sent)]))
        sent[-1].start()

    for i in range(2):
        send(rows_in.at[pl.ds(i * N, N), :], out_hbm.at[group_rows(2 * core + i, odd_row), :])

    def fetch(ref, k):
        return ref[pl.ds(k, N, stride=ROWS), :]

    diags = fetch(own, 3) + fetch(other, 3)
    first = fetch(other, 0)
    fifth = jnp.where(fifth_half == core, fetch(own, 1), fetch(other, 1))
    lane = 32 * (1 - core) + group + 4 * odd_row
    blocks = [unpacked(first, second, diags, lane) for second in range(2)]
    blocks.append(unpacked(fifth, odd_row, diags, 32 * fifth_half + 8 + group // 2))
    scalars.wait()
    block, slot_half, slot_place, slot_second = [number(meta, i) for i in range(4)]
    mine = jnp.where(slot_half == core, fetch(own, 4 + core), fetch(other, 4 + core))
    fresh = unpacked(mine, slot_second, diags, 32 * slot_half + slot_place)
    updated[0] = jnp.where(block > 0, fresh, 0.0)
    send(updated, updated_hbm)

    approx = inverses(blocks, meta[0, 4])
    right = [right_in[0], right_in[1]]
    for i in range(3):
        at = group_rows("fifth" if i == 2 else 2 * (1 - core) + i, odd_row)
        out[pl.ds(i * N, N), :] = both_sides(approx[i], weight[at, :], right)
        send(out.at[pl.ds(i * N, N), :], out_hbm.at[at, :])
    for copy in sent:
        copy.wait()


def apply_near(places, meta, own, weight):
    vmem, hbm = pl.BlockSpec(memory_space=pltpu.VMEM), pl.BlockSpec(memory_space=pltpu.HBM)
    return pl.pallas_call(
        functools.partial(near_kernel, places),
        out_shape=(
            jax.ShapeDtypeStruct((2 * N, 2 * N), jnp.float32),
            jax.ShapeDtypeStruct((2, 2 * N, 2 * N), jnp.bfloat16),
        ),
        in_specs=[hbm, vmem, vmem],
        out_specs=(vmem, vmem),
        scratch_shapes=[pltpu.SMEM((1, N), jnp.float32), pltpu.SemaphoreType.DMA((1,))],
        compiler_params=pltpu.CompilerParams(vmem_limit_bytes=40 * 2**20),
        name="apply_near",
    )(meta, own, weight)


def apply_far(places, meta, own, other, weight, rows, right):
    vmem, hbm = pl.BlockSpec(memory_space=pltpu.VMEM), pl.BlockSpec(memory_space=pltpu.HBM)
    return pl.pallas_call(
        functools.partial(far_kernel, places),
        out_shape=(
            jax.ShapeDtypeStruct(weight.shape, jnp.float32),
            jax.ShapeDtypeStruct((1, N, N), jnp.float32),
        ),
        in_specs=[hbm] + [vmem] * 5,
        out_specs=(hbm, hbm),
        scratch_shapes=[
            pltpu.VMEM((3 * N, 2 * N), jnp.float32),
            pltpu.VMEM((1, N, N), jnp.float32),
            pltpu.SMEM((1, N), jnp.float32),
            pltpu.SemaphoreType.DMA((1,)),
            pltpu.SemaphoreType.DMA((6,)),
        ],
        compiler_params=pltpu.CompilerParams(vmem_limit_bytes=40 * 2**20),
        name="apply_far",
    )(meta, own, other, weight, rows, right)


def on_device(acts, outgrads, weight_grad, prev_factor, damping, owner):
    core_of = lambda: lax.axis_index("c").astype(jnp.int32)
    row_of = lambda: lax.axis_index(("zh", "x")).astype(jnp.int32)
    col_of = lambda: lax.axis_index(("zl", "y", "c")).astype(jnp.int32)
    me_of = lambda: row_of() * 32 + col_of()

    places = (core_of, row_of, col_of)
    swap = [(0, 1), (1, 0)]
    other = partials(acts, outgrads, prev_factor, owner, core_of, me_of)
    received = lax.ppermute(other, "c", swap)
    own, picks, apply_meta = partials(acts, outgrads, prev_factor, owner, core_of, me_of, damping.reshape(1))
    chip = add_cores(own, received)

    got = lax.all_to_all(chip.reshape(16, 8 * TILES, N), PLANE, 0, 0, tiled=True)
    by_depth = plane_sum(got)
    got = lax.all_to_all(by_depth, DEPTH, 0, 0, tiled=True)
    sent = spread_rows(got, picks)
    near = lax.all_to_all(sent.reshape(N, ROWS, 1, N), CHIPS, 0, 0, tiled=True).reshape(ROWS * N, N)
    far = lax.ppermute(near, "c", swap)
    rows, right = apply_near(places, apply_meta, near, weight_grad)
    return apply_far(places, apply_meta, near, far, weight_grad, rows, right)


def solution(mesh):
    fine = Mesh(mesh.devices.reshape(2, 4, 4, 4, 2), ALL)
    row, col = ("zh", "x"), ("zl", "y", "c")
    placed = (P(ALL, None), P(ALL, None), P(row, col), P(ALL, None, None), P(), P())
    return jax.shard_map(
        on_device,
        mesh=fine,
        in_specs=placed,
        out_specs=(P(row, col), P(ALL, None, None)),
        check_vma=False,
    )
```
